32 devices in a mesh: dp: 16 (over z, x, core), mp: 2 (over y).
Axes of the slice: x: 2, y: 2, z: 4, core: 2. Of those that a mesh axis runs over, the one named last changes fastest.
Arguments:
- acc_grads: bfloat16 [16, 2, 128, 49152], P('dp', None, None, 'mp'), may hold values from -6 to 6
- activations: bfloat16 [2048, 2, 128], P('dp')
- cotangent: bfloat16 [2048, 2, 49152], P('dp', None, 'mp')
- params: float32 [2, 128, 49152], P(None, 'dp', 'mp'), may hold values from -6 to 6
- first_moment: float32 [2, 128, 49152], P(None, 'dp', 'mp'), may hold values from -4 to 4
- second_moment: float32 [2, 128, 49152], P(None, 'dp', 'mp'), may hold values from 0.25 to 1
- step: int32 [1], replicated, may hold values from 1 to 16
Outputs:
- new_params: float32 [2, 128, 49152], P(None, 'dp', 'mp')
- new_first: float32 [2, 128, 49152], P(None, 'dp', 'mp')
- new_second: float32 [2, 128, 49152], P(None, 'dp', 'mp')
- copy_params: float32 [2, 128, 49152], P(None, 'dp', 'mp')
- copy_first: float32 [2, 128, 49152], P(None, 'dp', 'mp')
- copy_second: float32 [2, 128, 49152], P(None, 'dp', 'mp')
The draws below stay inside these ranges and needn't reach their ends.
All inputs are finite; a program needn't handle non-finite values.
Results may differ from the reference program's by a relative error of at most 0.0014.
Values sent between devices are 32-bit elements; how exact they have to be, the bound alone decides.
No kernel may reach another device: no remote copies, remote signals or barrier semaphores. Data moves between devices by JAX's collectives and lax.ppermute only.
A program may use at most 128 MiB of HBM per device.

```python
import math
import jax
import jax.numpy as jnp
from jax import lax

HID = 49152
LAYERS = 2
ROWS_DEV = 8
TOK_DEV = 128
ROWS = 128
TOKENS = 2048
N_DP = 16


def draw_activations(key, part):
    values = jax.random.normal(key, (TOKENS, LAYERS, ROWS), jnp.float32)
    position = jnp.arange(ROWS, dtype=jnp.float32) / max(ROWS - 1, 1)
    scales = jnp.exp(math.log(10.0) * position)
    return (values * scales).astype(jnp.bfloat16)


def draw_cotangent(key, part):
    first_key = jax.random.fold_in(key, 11)
    second_key = jax.random.fold_in(key, 12)
    values = jax.random.normal(first_key, (TOKENS, LAYERS, HID), jnp.float32)
    scales = jnp.exp(jax.random.uniform(second_key, (1, LAYERS, HID), jnp.float32, 0.0, math.log(10.0)))
    return (0.003 * values * scales).astype(jnp.bfloat16)


def raised(drawn, own_key, source, target, blocks, factor):
    owner, partner = [(jnp.arange(drawn.shape[dim]) // (drawn.shape[dim] // blocks)).reshape([-1 if axis == dim else 1 for axis in range(drawn.ndim)]) for dim in (source, target)]
    chosen = jax.random.permutation(own_key, blocks)[partner]
    strong = (owner == chosen) | (owner == (partner + blocks // 2) % blocks)
    return jnp.where(strong, factor * drawn, drawn)


def levels(key, dims, cuts, least, high):
    factor_of = 1.0
    for dim, blocks in cuts:
        heights = jax.random.uniform(jax.random.fold_in(jax.random.fold_in(key, 6), dim), (blocks,), jnp.float32, least / len(cuts), high / len(cuts))
        factor_of = factor_of * jnp.repeat(jnp.exp(heights), dims[dim] // blocks).reshape((-1,) + (1,) * (len(dims) - 1 - dim))
    return factor_of


def bell_draw(rng, shape, width, limit, cuts=(), kind=jnp.bfloat16):
    drawn = jax.random.normal(rng, shape, jnp.float32) * width
    if len(cuts) > 0:
        drawn = levels(rng, shape, cuts, -0.22, 0.18) * drawn
    return jnp.clip(drawn, min=-limit, max=limit).astype(kind)


def heavy_noise(rng, dims, deviation, most, shards, heavy, kind=jnp.bfloat16):
    entries = deviation * jax.random.normal(rng, dims, jnp.float32)
    if shards:
        entries = entries * levels(rng, dims, shards, -0.22, 0.18)
    return jnp.clip(raised(entries, jax.random.fold_in(rng, 3), *heavy), -most, most).astype(kind)


def setup_inputs(seed: int = 0) -> dict:
    key_list = jax.random.split(jax.random.key(seed), 8)
    return {
        "acc_grads": heavy_noise(key_list[0], (N_DP, LAYERS, ROWS, HID), 0.3, 6.0, ((0, 16), (3, 2)), (0, 2, 16, 2.0)),
        "activations": draw_activations(jax.random.fold_in(key_list[7], 71), 0),
        "cotangent": draw_cotangent(jax.random.fold_in(key_list[7], 71), 0),
        "params": bell_draw(key_list[3], (LAYERS, ROWS, HID), 1.0, 6.0, ((1, 16), (2, 2)), jnp.float32),
        "first_moment": bell_draw(key_list[4], (LAYERS, ROWS, HID), 0.5, 4.0, ((1, 16), (2, 2)), jnp.float32),
        "second_moment": jnp.clip(jnp.exp(math.log(1.0) - 1.3862944 * jax.random.uniform(key_list[5], (LAYERS, ROWS, HID), jnp.float32) ** levels(key_list[5], (LAYERS, ROWS, HID), ((1, 16), (2, 2)), -0.2, 0.2)), 0.25, 1.0),
        "step": jax.random.randint(key_list[6], (1,), 1, 17).astype(jnp.int32),
    }


beta_one = 0.9
beta_two = 0.95
learn_rate = 0.1
decay_rate = 0.1
epsilon = 1e-08

def adamw_update(weights, first, second, grad, factor, count):
    scaled = factor * grad
    first_new = beta_one * first + (1.0 - beta_one) * scaled
    second_new = beta_two * second + (1.0 - beta_two) * scaled * scaled
    first_hat = first_new / (1.0 - jnp.power(jnp.float32(beta_one), count))
    second_hat = second_new / (1.0 - jnp.power(jnp.float32(beta_two), count))
    weights_new = weights - learn_rate * (first_hat / (jnp.sqrt(second_hat) + epsilon) + decay_rate * weights)
    return (weights_new, first_new, second_new)

def reference(acc_grads, activations, cotangent, params, first_moment, second_moment, step):

    def member(total, index):
        start = (index * TOK_DEV).astype(jnp.int32)
        inputs = lax.dynamic_slice_in_dim(activations, start, TOK_DEV, 0).astype(jnp.float32)
        outgrad = lax.dynamic_slice_in_dim(cotangent, start, TOK_DEV, 0).astype(jnp.float32)
        product = jnp.einsum('tlr,tlc->lrc', inputs, outgrad)
        earlier = lax.dynamic_index_in_dim(acc_grads, index, 0, keepdims=False).astype(jnp.float32)
        local_sum = lax.optimization_barrier((earlier + product).astype(jnp.bfloat16))
        return (total + local_sum.astype(jnp.float32), None)
    start_total = jnp.zeros((LAYERS, ROWS, HID), jnp.float32)
    grad, _ = lax.scan(member, start_total, jnp.arange(N_DP, dtype=jnp.int32))
    norm = jnp.sqrt(jnp.sum(grad * grad))
    bound = jnp.sqrt(jnp.float32(LAYERS * ROWS * HID))
    factor = jnp.minimum(jnp.float32(1.0), bound / (norm + 1e-06))
    count = step[0].astype(jnp.float32)
    new_params, new_first, new_second = adamw_update(params, first_moment, second_moment, grad, factor, count)
    copy_params = jnp.roll(new_params, ROWS_DEV, axis=1)
    copy_first = jnp.roll(new_first, ROWS_DEV, axis=1)
    copy_second = jnp.roll(new_second, ROWS_DEV, axis=1)
    return (new_params, new_first, new_second, copy_params, copy_first, copy_second)
```

```python
import functools

import jax
import jax.numpy as jnp
from jax import lax
from jax.experimental import pallas as pl
from jax.experimental.pallas import tpu as pltpu
from jax.sharding import PartitionSpec as P

beta_one = 0.9
beta_two = 0.95
learn_rate = 0.1
decay_rate = 0.1
epsilon = 1e-08

streams = 4
lanes = 128
room = pltpu.CompilerParams(vmem_limit_bytes=48 * 2**20)


def block_of(columns, most):
    best = lanes
    for size in range(lanes, min(columns, most) + 1, lanes):
        if columns % size == 0:
            best = size
    return best


def adamw_update(weights, first, second, grad, factor, first_scale, second_scale):
    scaled = factor * grad
    first_new = beta_one * first + (1.0 - beta_one) * scaled
    second_new = beta_two * second + (1.0 - beta_two) * scaled * scaled
    first_hat = first_new / first_scale
    second_hat = second_new / second_scale
    weights_new = weights - learn_rate * (
        first_hat / (jnp.sqrt(second_hat) + epsilon) + decay_rate * weights
    )
    return (weights_new, first_new, second_new)


def terms_kernel(order, layers, core_ref, inputs_ref, earlier_ref, outgrad_ref, keep_ref, give_ref):
    core = core_ref[0]
    tokens, _, columns = outgrad_ref.shape
    rows = earlier_ref.shape[2]
    outgrad = outgrad_ref[...].reshape(tokens * layers, columns)
    product = jnp.dot(inputs_ref[...], outgrad, preferred_element_type=jnp.float32)
    chips = len(order)
    for layer in range(layers):
        total = earlier_ref[0, layer].astype(jnp.float32) + product[layer * rows : (layer + 1) * rows]
        term = total.astype(jnp.bfloat16).astype(jnp.float32)
        term = term.reshape(chips, 2, rows // (2 * chips), columns)
        for place, chip in enumerate(order):
            keep_ref[place, layer] = jnp.where(core == 0, term[chip, 0], term[chip, 1])
            give_ref[place, layer] = jnp.where(core == 0, term[chip, 1], term[chip, 0])


def make_terms(core, inputs, earlier, outgrad, order, start, width):
    _, layers, rows, _ = earlier.shape
    tokens = outgrad.shape[0]
    chips = len(order)
    own = rows // (2 * chips)
    size = block_of(width, 2048)
    first = start // size
    return pl.pallas_call(
        functools.partial(terms_kernel, order, layers),
        grid_spec=pltpu.PrefetchScalarGridSpec(
            num_scalar_prefetch=1,
            grid=(width // size,),
            in_specs=[
                pl.BlockSpec(inputs.shape, lambda i, core: (0, 0)),
                pl.BlockSpec((1, layers, rows, size), lambda i, core: (0, 0, 0, first + i)),
                pl.BlockSpec((tokens, layers, size), lambda i, core: (0, 0, first + i)),
            ],
            out_specs=[pl.BlockSpec((chips, layers, own, size), lambda i, core: (0, 0, 0, i))] * 2,
        ),
        out_shape=[jax.ShapeDtypeStruct((chips, layers, own, width), jnp.float32)] * 2,
        compiler_params=room,
        name="terms",
    )(core, inputs, earlier, outgrad)


def first_kernel(shard_ref, keep_ref, theirs_ref, out_ref):
    out_ref[...] = keep_ref[0] + theirs_ref[0]


def step_kernel(shard_ref, keep_ref, theirs_ref, arrived_ref, out_ref):
    out_ref[...] = arrived_ref[...] + (keep_ref[0] + theirs_ref[0])


def last_kernel(shard_ref, keep_ref, theirs_ref, arrived_ref, out_ref, squares_ref):
    grad = arrived_ref[...] + (keep_ref[0] + theirs_ref[0])
    out_ref[...] = grad
    layers, own, columns = grad.shape
    squares = jnp.sum((grad * grad).reshape(layers, own, columns // lanes, lanes), axis=(0, 2))

    @pl.when(pl.program_id(0) == 0)
    def _():
        squares_ref[...] = squares

    @pl.when(pl.program_id(0) > 0)
    def _():
        squares_ref[...] += squares


def ring_add(shards, step, keep, theirs, arrived, last):
    _, layers, own, width = keep.shape
    size = block_of(width, 3072)
    chosen = pl.BlockSpec((1, layers, own, size), lambda i, shards: (shards[step], 0, 0, i))
    whole = pl.BlockSpec((layers, own, size), lambda i, shards: (0, 0, i))
    summed = jax.ShapeDtypeStruct((layers, own, width), jnp.float32)
    out_shape, out_specs = summed, whole
    body = step_kernel
    if arrived is None:
        body = first_kernel
    elif last:
        body = last_kernel
        out_shape = [summed, jax.ShapeDtypeStruct((own, lanes), jnp.float32)]
        out_specs = [whole, pl.BlockSpec((own, lanes), lambda i, shards: (0, 0))]
    rest = [] if arrived is None else [arrived]
    return pl.pallas_call(
        body,
        grid_spec=pltpu.PrefetchScalarGridSpec(
            num_scalar_prefetch=1,
            grid=(width // size,),
            in_specs=[chosen, chosen] + [whole] * len(rest),
            out_specs=out_specs,
        ),
        out_shape=out_shape,
        compiler_params=room,
        name="ring_add",
    )(shards, keep, theirs, *rest)


def update_kernel(count, bound, scales_ref, squares_ref, weights_ref, first_ref, second_ref, *rest):
    grads, outs = rest[:count], rest[count:]
    step = pl.program_id(0)
    per = pl.num_programs(0) // count
    factor = jnp.minimum(
        jnp.float32(1.0), bound / (jnp.sqrt(jnp.sum(squares_ref[...])) + jnp.float32(1e-06))
    )
    for index, grad_ref in enumerate(grads):

        @pl.when(step // per == index)
        def _(grad_ref=grad_ref):
            new = adamw_update(
                weights_ref[...],
                first_ref[...],
                second_ref[...],
                grad_ref[...],
                factor,
                scales_ref[0],
                scales_ref[1],
            )
            for out_ref, value in zip(outs, new):
                out_ref[...] = value


def update(scales, squares, state, grads, bound):
    layers, own, columns = state[0].shape
    width = grads[0].shape[-1]
    count = len(grads)
    size = block_of(width, 3072)
    per = width // size
    block = pl.BlockSpec((layers, own, size), lambda i: (0, 0, i))
    return pl.pallas_call(
        functools.partial(update_kernel, count, bound),
        grid=(columns // size,),
        in_specs=[
            pl.BlockSpec(memory_space=pltpu.SMEM),
            pl.BlockSpec(squares.shape, lambda i: (0, 0)),
        ]
        + [block] * 3
        + [
            pl.BlockSpec(
                (layers, own, size), lambda i, k=k: (0, 0, jnp.clip(i - k * per, 0, per - 1))
            )
            for k in range(count)
        ],
        out_specs=[block] * 3,
        out_shape=[jax.ShapeDtypeStruct((layers, own, columns), jnp.float32)] * 3,
        compiler_params=room,
        name="update",
    )(scales, squares, *state, *grads)


def total_over(value, axis):
    peers = lax.axis_size(axis)
    if peers & (peers - 1):
        return lax.psum(value, axis)
    bit = 1
    while bit < peers:
        value = value + lax.ppermute(value, axis, [(i, i ^ bit) for i in range(peers)])
        bit *= 2
    return value


def local(acc_grads, activations, cotangent, params, first_moment, second_moment, step):
    _, layers, rows, columns = acc_grads.shape
    tokens = activations.shape[0]
    peers = lax.axis_size("dp")
    chips = peers // 2
    half = chips // 2
    order = [2 * z for z in range(half)] + [2 * z + 1 for z in reversed(range(half))]
    forward = [
        (2 * order[r] + core, 2 * order[(r + 1) % chips] + core)
        for r in range(chips)
        for core in range(2)
    ]
    backward = [(target, source) for source, target in forward]
    swap = [(i, i ^ 1) for i in range(peers)]
    onward = [(i, (i + 1) % peers) for i in range(peers)]

    index = lax.axis_index("dp")
    core, chip = index % 2, index // 2
    place = jnp.where(chip % 2 == 0, chip // 2, chips - 1 - chip // 2)
    hops = jnp.arange(1, chips + 1, dtype=jnp.int32)
    shards = [jnp.mod(place - hops, chips), jnp.mod(place + hops, chips)]
    core = core.reshape(1)

    state = (params, first_moment, second_moment)
    old_copy = [lax.ppermute(value, "dp", onward) for value in state]

    same = jnp.eye(layers, dtype=activations.dtype)
    inputs = activations.transpose(1, 2, 0)[:, :, :, None] * same[:, None, None, :]
    inputs = inputs.reshape(layers * rows, tokens * layers)

    width = columns // streams
    keep, theirs = [], []
    for k in range(streams):
        mine, give = make_terms(core, inputs, acc_grads, cotangent, order, k * width, width)
        keep.append(mine)
        theirs.append(lax.ppermute(give, "dp", swap))

    sums = [None] * streams
    squares = None
    for hop in range(chips):
        for k in range(streams):
            last = hop == chips - 1
            out = ring_add(shards[k % 2], hop, keep[k], theirs[k], sums[k], last)
            if last:
                sums[k], part = out
                squares = part if squares is None else squares + part
            else:
                sums[k] = lax.ppermute(out, "dp", backward if k % 2 else forward)

    peer_grads = [lax.ppermute(value, "dp", onward) for value in sums]
    squares = total_over(total_over(squares, "dp"), "mp")
    bound = float((layers * rows * columns * lax.axis_size("mp")) ** 0.5)
    count = step.astype(jnp.float32)
    scales = jnp.concatenate(
        [
            1.0 - jnp.power(jnp.float32(beta_one), count),
            1.0 - jnp.power(jnp.float32(beta_two), count),
        ]
    )
    new = update(scales, squares, state, sums, bound)
    copies = update(scales, squares, old_copy, peer_grads, bound)
    return (*new, *copies)


def solution(mesh):
    owned = P(None, "dp", "mp")
    return jax.shard_map(
        local,
        mesh=mesh,
        in_specs=(
            P("dp", None, None, "mp"),
            P("dp", None, None),
            P("dp", None, "mp"),
            owned,
            owned,
            owned,
            P(),
        ),
        out_specs=(owned,) * 6,
        check_vma=False,
    )
```

```python
import functools
import math

import jax
import jax.numpy as jnp
from jax import lax
from jax.experimental import pallas as pl
from jax.experimental.pallas import tpu as pltpu
from jax.sharding import PartitionSpec as P

beta_one = 0.9
beta_two = 0.95
learn_rate = 0.1
decay_rate = 0.1
epsilon = 1e-08

streams = 2
lanes = 128
room = pltpu.CompilerParams(vmem_limit_bytes=48 * 2**20)


def block_of(columns, most):
    best = lanes
    for size in range(lanes, min(columns, most) + 1, lanes):
        if columns % size == 0:
            best = size
    return best


def cost_of(*arrays):
    moved = sum(math.prod(a.shape) * jnp.dtype(a.dtype).itemsize for a in arrays)
    return pl.CostEstimate(flops=0, bytes_accessed=moved, transcendentals=0)


def adamw_update(weights, first, second, grad, factor, first_scale, second_scale):
    scaled = factor * grad
    first_new = beta_one * first + (1.0 - beta_one) * scaled
    second_new = beta_two * second + (1.0 - beta_two) * scaled * scaled
    first_hat = first_new / first_scale
    second_hat = second_new / second_scale
    weights_new = weights - learn_rate * (
        first_hat / (jnp.sqrt(second_hat) + epsilon) + decay_rate * weights
    )
    return (weights_new, first_new, second_new)


def terms_kernel(order, layers, core_ref, inputs_ref, earlier_ref, outgrad_ref, keep_ref, give_ref):
    core = core_ref[0]
    tokens, _, columns = outgrad_ref.shape
    rows = earlier_ref.shape[2]
    outgrad = outgrad_ref[...].reshape(tokens * layers, columns)
    product = jnp.dot(inputs_ref[...], outgrad, preferred_element_type=jnp.float32)
    chips = len(order)
    for layer in range(layers):
        total = earlier_ref[0, layer].astype(jnp.float32) + product[layer * rows : (layer + 1) * rows]
        term = total.astype(jnp.bfloat16).astype(jnp.float32)
        term = term.reshape(chips, 2, rows // (2 * chips), columns)
        for place, chip in enumerate(order):
            keep_ref[place, layer] = jnp.where(core == 0, term[chip, 0], term[chip, 1])
            give_ref[place, layer] = jnp.where(core == 0, term[chip, 1], term[chip, 0])


def make_terms(core, inputs, earlier, outgrad, order, start, width):
    _, layers, rows, _ = earlier.shape
    tokens = outgrad.shape[0]
    chips = len(order)
    own = rows // (2 * chips)
    size = block_of(width, 2048)
    first = start // size
    return pl.pallas_call(
        functools.partial(terms_kernel, order, layers),
        grid_spec=pltpu.PrefetchScalarGridSpec(
            num_scalar_prefetch=1,
            grid=(width // size,),
            in_specs=[
                pl.BlockSpec(inputs.shape, lambda i, core: (0, 0)),
                pl.BlockSpec((1, layers, rows, size), lambda i, core: (0, 0, 0, first + i)),
                pl.BlockSpec((tokens, layers, size), lambda i, core: (0, 0, first + i)),
            ],
            out_specs=[pl.BlockSpec((chips, layers, own, size), lambda i, core: (0, 0, 0, i))] * 2,
        ),
        out_shape=[jax.ShapeDtypeStruct((chips, layers, own, width), jnp.float32)] * 2,
        compiler_params=room,
        cost_estimate=cost_of(
            jax.ShapeDtypeStruct((layers, rows + tokens, width), earlier.dtype),
            jax.ShapeDtypeStruct((layers, rows, width), jnp.float32),
        ),
        name="terms",
    )(core, inputs, earlier, outgrad)


def plain_kernel(shard_ref, keep_ref, theirs_ref, *rest):
    out_ref = rest[-1]
    out_ref[...] = keep_ref[0] + theirs_ref[0]


def step_kernel(shard_ref, keep_ref, theirs_ref, arrived_ref, *rest):
    out_ref = rest[-1]
    out_ref[...] = arrived_ref[...] + (keep_ref[0] + theirs_ref[0])


def last_kernel(shard_ref, keep_ref, theirs_ref, up_ref, down_ref, *rest):
    out_ref, squares_ref = rest[-2:]
    grad = (up_ref[...] + down_ref[...]) + (keep_ref[0] + theirs_ref[0])
    out_ref[...] = grad
    layers, own, columns = grad.shape
    squares = jnp.sum((grad * grad).reshape(layers, own, columns // lanes, lanes), axis=(0, 2))

    @pl.when(pl.program_id(0) == 0)
    def _():
        squares_ref[...] = squares

    @pl.when(pl.program_id(0) > 0)
    def _():
        squares_ref[...] += squares


def shard_sum(body, shards, which, keep, theirs, *arrived, after=()):
    _, layers, own, width = keep.shape
    size = block_of(width, 3072)
    chosen = pl.BlockSpec((1, layers, own, size), lambda i, shards: (shards[which], 0, 0, i))
    whole = pl.BlockSpec((layers, own, size), lambda i, shards: (0, 0, i))
    summed = jax.ShapeDtypeStruct((layers, own, width), jnp.float32)
    out_shape, out_specs = summed, whole
    if body is last_kernel:
        out_shape = [summed, jax.ShapeDtypeStruct((own, lanes), jnp.float32)]
        out_specs = [whole, pl.BlockSpec((own, lanes), lambda i, shards: (0, 0))]
    return pl.pallas_call(
        body,
        grid_spec=pltpu.PrefetchScalarGridSpec(
            num_scalar_prefetch=1,
            grid=(width // size,),
            in_specs=[chosen, chosen]
            + [whole] * len(arrived)
            + [pl.BlockSpec(memory_space=pl.ANY)] * len(after),
            out_specs=out_specs,
        ),
        out_shape=out_shape,
        compiler_params=room,
        cost_estimate=cost_of(*[summed] * (3 + len(arrived))),
        name="shard_sum",
    )(shards, keep, theirs, *arrived, *after)


def update_kernel(count, bound, scales_ref, squares_ref, weights_ref, first_ref, second_ref, *rest):
    grads, outs = rest[:count], rest[count:]
    step = pl.program_id(0)
    per = pl.num_programs(0) // count
    factor = jnp.minimum(
        jnp.float32(1.0), bound / (jnp.sqrt(jnp.sum(squares_ref[...])) + jnp.float32(1e-06))
    )
    for index, grad_ref in enumerate(grads):

        @pl.when(step // per == index)
        def _(grad_ref=grad_ref):
            new = adamw_update(
                weights_ref[...],
                first_ref[...],
                second_ref[...],
                grad_ref[...],
                factor,
                scales_ref[0],
                scales_ref[1],
            )
            for out_ref, value in zip(outs, new):
                out_ref[...] = value


def update(scales, squares, state, grads, bound):
    layers, own, columns = state[0].shape
    width = grads[0].shape[-1]
    count = len(grads)
    size = block_of(width, 3072)
    per = width // size
    block = pl.BlockSpec((layers, own, size), lambda i: (0, 0, i))
    return pl.pallas_call(
        functools.partial(update_kernel, count, bound),
        grid=(columns // size,),
        in_specs=[
            pl.BlockSpec(memory_space=pltpu.SMEM),
            pl.BlockSpec(squares.shape, lambda i: (0, 0)),
        ]
        + [block] * 3
        + [
            pl.BlockSpec(
                (layers, own, size), lambda i, k=k: (0, 0, jnp.clip(i - k * per, 0, per - 1))
            )
            for k in range(count)
        ],
        out_specs=[block] * 3,
        out_shape=[jax.ShapeDtypeStruct((layers, own, columns), jnp.float32)] * 3,
        compiler_params=room,
        cost_estimate=cost_of(*[state[0]] * 7),
        name="update",
    )(scales, squares, *state, *grads)


def total_over(value, axis):
    peers = lax.axis_size(axis)
    if peers & (peers - 1):
        return lax.psum(value, axis)
    bit = 1
    while bit < peers:
        value = value + lax.ppermute(value, axis, [(i, i ^ bit) for i in range(peers)])
        bit *= 2
    return value


def local(acc_grads, activations, cotangent, params, first_moment, second_moment, step):
    _, layers, rows, columns = acc_grads.shape
    tokens = activations.shape[0]
    peers = lax.axis_size("dp")
    chips = peers // 2
    half = chips // 2
    order = [2 * z for z in range(half)] + [2 * z + 1 for z in reversed(range(half))]

    def hop(by):
        return [
            (2 * order[r] + core, 2 * order[(r + by) % chips] + core)
            for r in range(chips)
            for core in range(2)
        ]

    swap = [(i, i ^ 1) for i in range(peers)]
    onward = [(i, (i + 1) % peers) for i in range(peers)]

    index = lax.axis_index("dp")
    core, chip = index % 2, index // 2
    place = jnp.where(chip % 2 == 0, chip // 2, chips - 1 - chip // 2)
    hops = jnp.arange(half + 1, dtype=jnp.int32)
    tables = [
        jnp.concatenate([jnp.mod(place + by * hops, chips), core.reshape(1)]) for by in (1, -1)
    ]

    state = (params, first_moment, second_moment)
    old_copy = [lax.ppermute(value, "dp", onward) for value in state]

    same = jnp.eye(layers, dtype=activations.dtype)
    inputs = activations.transpose(1, 2, 0)[:, :, :, None] * same[:, None, None, :]
    inputs = inputs.reshape(layers * rows, tokens * layers)

    width = columns // streams
    keep, theirs, sent, grads, peer_grads = ([None] * streams for _ in range(5))
    for k in range(streams):
        keep[k], give = make_terms(
            core.reshape(1), inputs, acc_grads, cotangent, order, k * width, width
        )
        theirs[k] = lax.ppermute(give, "dp", swap)
    for k in range(streams):
        total = shard_sum(plain_kernel, tables[0], half, keep[k], theirs[k], after=old_copy[k : k + 1])
        sent[k] = [None, None]
        sent[k][k % 2] = lax.ppermute(total, "dp", hop(-1 if k % 2 else 1))
    waiting = old_copy[streams:]
    for away in range(half - 1, 0, -1):
        for k in range(streams):
            for way, by in enumerate((1, -1)):
                arrived, after = [], ()
                if sent[k][way] is not None:
                    arrived, after, waiting = [sent[k][way]], waiting, ()
                body = step_kernel if arrived else plain_kernel
                total = shard_sum(
                    body, tables[way], away, keep[k], theirs[k], *arrived, after=after
                )
                sent[k][way] = lax.ppermute(total, "dp", hop(by))
    squares = None
    for k in range(streams):
        grads[k], part = shard_sum(last_kernel, tables[0], 0, keep[k], theirs[k], *sent[k])
        peer_grads[k] = lax.ppermute(grads[k], "dp", onward)
        squares = part if squares is None else squares + part

    squares = total_over(total_over(squares, "dp"), "mp")
    bound = float((layers * rows * columns * lax.axis_size("mp")) ** 0.5)
    count = step.astype(jnp.float32)
    scales = jnp.concatenate(
        [
            1.0 - jnp.power(jnp.float32(beta_one), count),
            1.0 - jnp.power(jnp.float32(beta_two), count),
        ]
    )
    new = update(scales, squares, state, grads, bound)
    copies = update(scales, squares, old_copy, peer_grads, bound)
    return (*new, *copies)


def solution(mesh):
    owned = P(None, "dp", "mp")
    return jax.shard_map(
        local,
        mesh=mesh,
        in_specs=(
            P("dp", None, None, "mp"),
            P("dp", None, None),
            P("dp", None, "mp"),
            owned,
            owned,
            owned,
            P(),
        ),
        out_specs=(owned,) * 6,
        check_vma=False,
    )
```

```python
import functools
import math

import jax
import jax.numpy as jnp
from jax import lax
from jax.experimental import pallas as pl
from jax.experimental.pallas import tpu as pltpu
from jax.sharding import PartitionSpec as P

beta_one = 0.9
beta_two = 0.95
learn_rate = 0.1
decay_rate = 0.1
epsilon = 1e-08

streams = 2
lanes = 128
room = pltpu.CompilerParams(vmem_limit_bytes=60 * 2**20)


def block_of(columns, most):
    best = lanes
    for size in range(lanes, min(columns, most) + 1, lanes):
        if columns % size == 0:
            best = size
    return best


def cost_of(*arrays):
    moved = sum(math.prod(a.shape) * jnp.dtype(a.dtype).itemsize for a in arrays)
    return pl.CostEstimate(flops=0, bytes_accessed=moved, transcendentals=0)


def adamw_update(weights, first, second, grad, factor, first_scale, second_scale):
    scaled = factor * grad
    first_new = beta_one * first + (1.0 - beta_one) * scaled
    second_new = beta_two * second + (1.0 - beta_two) * scaled * scaled
    first_hat = first_new / first_scale
    second_hat = second_new / second_scale
    weights_new = weights - learn_rate * (
        first_hat / (jnp.sqrt(second_hat) + epsilon) + decay_rate * weights
    )
    return (weights_new, first_new, second_new)


def terms_kernel(order, layers, core_ref, inputs_ref, earlier_ref, outgrad_ref, *rest):
    keep_ref, give_ref = rest[-2:]
    core = core_ref[0]
    tokens, _, columns = outgrad_ref.shape
    rows = earlier_ref.shape[2]
    outgrad = outgrad_ref[...].reshape(tokens * layers, columns)
    product = jnp.dot(inputs_ref[...], outgrad, preferred_element_type=jnp.float32)
    chips = len(order)
    for layer in range(layers):
        total = earlier_ref[0, layer].astype(jnp.float32) + product[layer * rows : (layer + 1) * rows]
        term = total.astype(jnp.bfloat16).astype(jnp.float32)
        term = term.reshape(chips, 2, rows // (2 * chips), columns)
        for place, chip in enumerate(order):
            keep_ref[place, layer] = jnp.where(core == 0, term[chip, 0], term[chip, 1])
            give_ref[place, layer] = jnp.where(core == 0, term[chip, 1], term[chip, 0])


def make_terms(core, inputs, earlier, outgrad, order, start, width, after=()):
    _, layers, rows, _ = earlier.shape
    tokens = outgrad.shape[0]
    chips = len(order)
    own = rows // (2 * chips)
    size = block_of(width, 6144)
    first = start // size
    return pl.pallas_call(
        functools.partial(terms_kernel, order, layers),
        grid_spec=pltpu.PrefetchScalarGridSpec(
            num_scalar_prefetch=1,
            grid=(width // size,),
            in_specs=[
                pl.BlockSpec(inputs.shape, lambda i, core: (0, 0)),
                pl.BlockSpec((1, layers, rows, size), lambda i, core: (0, 0, 0, first + i)),
                pl.BlockSpec((tokens, layers, size), lambda i, core: (0, 0, first + i)),
            ]
            + [pl.BlockSpec(memory_space=pl.ANY)] * len(after),
            out_specs=[pl.BlockSpec((chips, layers, own, size), lambda i, core: (0, 0, 0, i))] * 2,
        ),
        out_shape=[jax.ShapeDtypeStruct((chips, layers, own, width), jnp.float32)] * 2,
        compiler_params=room,
        cost_estimate=cost_of(
            jax.ShapeDtypeStruct((layers, rows + tokens, width), earlier.dtype),
            jax.ShapeDtypeStruct((layers, rows, width), jnp.float32),
        ),
        name="terms",
    )(core, inputs, earlier, outgrad, *after)


def plain_kernel(shard_ref, keep_ref, theirs_ref, *rest):
    out_ref = rest[-1]
    out_ref[...] = keep_ref[0] + theirs_ref[0]


def step_kernel(shard_ref, keep_ref, theirs_ref, arrived_ref, *rest):
    out_ref = rest[-1]
    out_ref[...] = arrived_ref[...] + (keep_ref[0] + theirs_ref[0])


def last_kernel(shard_ref, keep_ref, theirs_ref, up_ref, down_ref, *rest):
    out_ref, squares_ref = rest[-2:]
    grad = (up_ref[...] + down_ref[...]) + (keep_ref[0] + theirs_ref[0])
    out_ref[...] = grad
    layers, own, columns = grad.shape
    squares = jnp.sum((grad * grad).reshape(layers, own, columns // lanes, lanes), axis=(0, 2))

    @pl.when(pl.program_id(0) == 0)
    def _():
        squares_ref[...] = squares

    @pl.when(pl.program_id(0) > 0)
    def _():
        squares_ref[...] += squares


def shard_sum(body, shards, which, keep, theirs, *arrived, after=()):
    _, layers, own, width = keep.shape
    size = block_of(width, 6144)
    chosen = pl.BlockSpec((1, layers, own, size), lambda i, shards: (shards[which], 0, 0, i))
    whole = pl.BlockSpec((layers, own, size), lambda i, shards: (0, 0, i))
    summed = jax.ShapeDtypeStruct((layers, own, width), jnp.float32)
    out_shape, out_specs = summed, whole
    if body is last_kernel:
        out_shape = [summed, jax.ShapeDtypeStruct((own, lanes), jnp.float32)]
        out_specs = [whole, pl.BlockSpec((own, lanes), lambda i, shards: (0, 0))]
    return pl.pallas_call(
        body,
        grid_spec=pltpu.PrefetchScalarGridSpec(
            num_scalar_prefetch=1,
            grid=(width // size,),
            in_specs=[chosen, chosen]
            + [whole] * len(arrived)
            + [pl.BlockSpec(memory_space=pl.ANY)] * len(after),
            out_specs=out_specs,
        ),
        out_shape=out_shape,
        compiler_params=room,
        cost_estimate=cost_of(*[summed] * (3 + len(arrived))),
        name="shard_sum",
    )(shards, keep, theirs, *arrived, *after)


def update_kernel(count, bound, scales_ref, squares_ref, weights_ref, first_ref, second_ref, *rest):
    grads, outs = rest[:count], rest[count:]
    step = pl.program_id(0)
    per = pl.num_programs(0) // count
    factor = jnp.minimum(
        jnp.float32(1.0), bound / (jnp.sqrt(jnp.sum(squares_ref[...])) + jnp.float32(1e-06))
    )
    for index, grad_ref in enumerate(grads):

        @pl.when(step // per == index)
        def _(grad_ref=grad_ref):
            new = adamw_update(
                weights_ref[...],
                first_ref[...],
                second_ref[...],
                grad_ref[...],
                factor,
                scales_ref[0],
                scales_ref[1],
            )
            for out_ref, value in zip(outs, new):
                out_ref[...] = value


def update(scales, squares, state, grads, bound):
    layers, own, columns = state[0].shape
    width = grads[0].shape[-1]
    count = len(grads)
    size = block_of(width, 12288)
    per = width // size
    block = pl.BlockSpec((layers, own, size), lambda i: (0, 0, i))
    return pl.pallas_call(
        functools.partial(update_kernel, count, bound),
        grid=(columns // size,),
        in_specs=[
            pl.BlockSpec(memory_space=pltpu.SMEM),
            pl.BlockSpec(squares.shape, lambda i: (0, 0)),
        ]
        + [block] * 3
        + [
            pl.BlockSpec(
                (layers, own, size), lambda i, k=k: (0, 0, jnp.clip(i - k * per, 0, per - 1))
            )
            for k in range(count)
        ],
        out_specs=[block] * 3,
        out_shape=[jax.ShapeDtypeStruct((layers, own, columns), jnp.float32)] * 3,
        compiler_params=room,
        cost_estimate=cost_of(*[state[0]] * 7),
        name="update",
    )(scales, squares, *state, *grads)


def total_over(value, axis):
    peers = lax.axis_size(axis)
    if peers & (peers - 1):
        return lax.psum(value, axis)
    bit = 1
    while bit < peers:
        value = value + lax.ppermute(value, axis, [(i, i ^ bit) for i in range(peers)])
        bit *= 2
    return value


def local(acc_grads, activations, cotangent, params, first_moment, second_moment, step):
    _, layers, rows, columns = acc_grads.shape
    tokens = activations.shape[0]
    peers = lax.axis_size("dp")
    chips = peers // 2
    half = chips // 2
    order = [2 * z for z in range(half)] + [2 * z + 1 for z in reversed(range(half))]

    def hop(by):
        return [
            (2 * order[r] + core, 2 * order[(r + by) % chips] + core)
            for r in range(chips)
            for core in range(2)
        ]

    swap = [(i, i ^ 1) for i in range(peers)]
    onward = [(i, (i + 1) % peers) for i in range(peers)]

    index = lax.axis_index("dp")
    core, chip = index % 2, index // 2
    place = jnp.where(chip % 2 == 0, chip // 2, chips - 1 - chip // 2)
    hops = jnp.arange(half + 1, dtype=jnp.int32)
    tables = [
        jnp.concatenate([jnp.mod(place + by * hops, chips), core.reshape(1)]) for by in (1, -1)
    ]

    state = (params, first_moment, second_moment)
    old_copy = [lax.ppermute(value, "dp", onward) for value in state]

    same = jnp.eye(layers, dtype=activations.dtype)
    inputs = activations.transpose(1, 2, 0)[:, :, :, None] * same[:, None, None, :]
    inputs = inputs.reshape(layers * rows, tokens * layers)

    width = columns // streams
    keep, theirs, sent, grads, peer_grads = ([None] * streams for _ in range(5))
    for k in range(streams):
        keep[k], give = make_terms(
            core.reshape(1), inputs, acc_grads, cotangent, order, k * width, width,
            after=old_copy[:1] if k == 1 else (),
        )
        theirs[k] = lax.ppermute(give, "dp", swap)
    for k in range(streams):
        total = shard_sum(plain_kernel, tables[0], half, keep[k], theirs[k], after=old_copy[1:2] if k == 1 else ())
        sent[k] = [None, None]
        sent[k][k % 2] = lax.ppermute(total, "dp", hop(-1 if k % 2 else 1))
    waiting = old_copy[2:]
    for away in range(half - 1, 0, -1):
        for k in range(streams):
            for way, by in enumerate((1, -1)):
                arrived, after = [], ()
                if sent[k][way] is not None:
                    arrived, after, waiting = [sent[k][way]], waiting, ()
                body = step_kernel if arrived else plain_kernel
                total = shard_sum(
                    body, tables[way], away, keep[k], theirs[k], *arrived, after=after
                )
                sent[k][way] = lax.ppermute(total, "dp", hop(by))
    squares = None
    for k in range(streams):
        grads[k], part = shard_sum(last_kernel, tables[0], 0, keep[k], theirs[k], *sent[k])
        peer_grads[k] = lax.ppermute(grads[k], "dp", onward)
        squares = part if squares is None else squares + part

    squares = total_over(total_over(squares, "dp"), "mp")
    bound = float((layers * rows * columns * lax.axis_size("mp")) ** 0.5)
    count = step.astype(jnp.float32)
    scales = jnp.concatenate(
        [
            1.0 - jnp.power(jnp.float32(beta_one), count),
            1.0 - jnp.power(jnp.float32(beta_two), count),
        ]
    )
    new = update(scales, squares, state, grads, bound)
    copies = update(scales, squares, old_copy, peer_grads, bound)
    return (*new, *copies)


def solution(mesh):
    owned = P(None, "dp", "mp")
    return jax.shard_map(
        local,
        mesh=mesh,
        in_specs=(
            P("dp", None, None, "mp"),
            P("dp", None, None),
            P("dp", None, "mp"),
            owned,
            owned,
            owned,
            P(),
        ),
        out_specs=(owned,) * 6,
        check_vma=False,
    )
```

```python
import functools
import math

import jax
import jax.numpy as jnp
from jax import lax
from jax.experimental import pallas as pl
from jax.experimental.pallas import tpu as pltpu
from jax.sharding import PartitionSpec as P

beta_one = 0.9
beta_two = 0.95
learn_rate = 0.1
decay_rate = 0.1
epsilon = 1e-08

streams = 2
lanes = 128
room = pltpu.CompilerParams(vmem_limit_bytes=60 * 2**20)


def block_of(columns, most):
    best = lanes
    for size in range(lanes, min(columns, most) + 1, lanes):
        if columns % size == 0:
            best = size
    return best


def cost_of(*arrays):
    moved = sum(math.prod(a.shape) * jnp.dtype(a.dtype).itemsize for a in arrays)
    return pl.CostEstimate(flops=0, bytes_accessed=moved, transcendentals=0)


def adamw_update(weights, first, second, grad, factor, first_scale, second_scale):
    scaled = factor * grad
    first_new = beta_one * first + (1.0 - beta_one) * scaled
    second_new = beta_two * second + (1.0 - beta_two) * scaled * scaled
    first_hat = first_new / first_scale
    second_hat = second_new / second_scale
    weights_new = weights - learn_rate * (
        first_hat / (jnp.sqrt(second_hat) + epsilon) + decay_rate * weights
    )
    return (weights_new, first_new, second_new)


def terms_kernel(order, layers, core_ref, inputs_ref, earlier_ref, outgrad_ref, *rest):
    keep_ref, gives = rest[-1 - layers], rest[-layers:]
    core = core_ref[0]
    tokens, _, columns = outgrad_ref.shape
    rows = earlier_ref.shape[2]
    outgrad = outgrad_ref[...].reshape(tokens * layers, columns)
    product = jnp.dot(inputs_ref[...], outgrad, preferred_element_type=jnp.float32)
    chips = len(order)
    for layer in range(layers):
        total = earlier_ref[0, layer].astype(jnp.float32) + product[layer * rows : (layer + 1) * rows]
        term = total.astype(jnp.bfloat16).astype(jnp.float32)
        term = term.reshape(chips, 2, rows // (2 * chips), columns)
        for place, chip in enumerate(order):
            keep_ref[place, layer] = jnp.where(core == 0, term[chip, 0], term[chip, 1])
            gives[layer][place] = jnp.where(core == 0, term[chip, 1], term[chip, 0])


def make_terms(core, inputs, earlier, outgrad, order, start, width):
    _, layers, rows, _ = earlier.shape
    tokens = outgrad.shape[0]
    chips = len(order)
    own = rows // (2 * chips)
    size = block_of(width, 6144)
    first = start // size
    return pl.pallas_call(
        functools.partial(terms_kernel, order, layers),
        grid_spec=pltpu.PrefetchScalarGridSpec(
            num_scalar_prefetch=1,
            grid=(width // size,),
            in_specs=[
                pl.BlockSpec(inputs.shape, lambda i, core: (0, 0)),
                pl.BlockSpec((1, layers, rows, size), lambda i, core: (0, 0, 0, first + i)),
                pl.BlockSpec((tokens, layers, size), lambda i, core: (0, 0, first + i)),
            ],
            out_specs=[pl.BlockSpec((chips, layers, own, size), lambda i, core: (0, 0, 0, i))]
            + [pl.BlockSpec((chips, own, size), lambda i, core: (0, 0, i))] * layers,
        ),
        out_shape=[jax.ShapeDtypeStruct((chips, layers, own, width), jnp.float32)]
        + [jax.ShapeDtypeStruct((chips, own, width), jnp.float32)] * layers,
        compiler_params=room,
        cost_estimate=cost_of(
            jax.ShapeDtypeStruct((layers, rows + tokens, width), earlier.dtype),
            jax.ShapeDtypeStruct((layers, rows, width), jnp.float32),
        ),
        name="terms",
    )(core, inputs, earlier, outgrad)


def both_cores(keep_ref, theirs):
    return jnp.stack([keep_ref[0, layer] + theirs_ref[0] for layer, theirs_ref in enumerate(theirs)])


def plain_kernel(layers, shard_ref, keep_ref, *rest):
    theirs, out_ref = rest[:layers], rest[-1]
    out_ref[...] = both_cores(keep_ref, theirs)


def step_kernel(layers, shard_ref, keep_ref, *rest):
    theirs, arrived_ref, out_ref = rest[:layers], rest[layers], rest[-1]
    out_ref[...] = arrived_ref[...] + both_cores(keep_ref, theirs)


def last_kernel(layers, shard_ref, keep_ref, *rest):
    theirs, up_ref, down_ref = rest[:layers], rest[layers], rest[layers + 1]
    out_ref, squares_ref = rest[-2:]
    grad = (up_ref[...] + down_ref[...]) + both_cores(keep_ref, theirs)
    out_ref[...] = grad
    _, own, columns = grad.shape
    squares = jnp.sum((grad * grad).reshape(layers, own, columns // lanes, lanes), axis=(0, 2))

    @pl.when(pl.program_id(0) == 0)
    def _():
        squares_ref[...] = squares

    @pl.when(pl.program_id(0) > 0)
    def _():
        squares_ref[...] += squares


def shard_sum(body, shards, which, keep, theirs, *arrived, after=()):
    _, layers, own, width = keep.shape
    size = block_of(width, 6144)
    chosen = pl.BlockSpec((1, layers, own, size), lambda i, shards: (shards[which], 0, 0, i))
    layer = pl.BlockSpec((1, own, size), lambda i, shards: (shards[which], 0, i))
    whole = pl.BlockSpec((layers, own, size), lambda i, shards: (0, 0, i))
    summed = jax.ShapeDtypeStruct((layers, own, width), jnp.float32)
    out_shape, out_specs = summed, whole
    if body is last_kernel:
        out_shape = [summed, jax.ShapeDtypeStruct((own, lanes), jnp.float32)]
        out_specs = [whole, pl.BlockSpec((own, lanes), lambda i, shards: (0, 0))]
    return pl.pallas_call(
        functools.partial(body, layers),
        grid_spec=pltpu.PrefetchScalarGridSpec(
            num_scalar_prefetch=1,
            grid=(width // size,),
            in_specs=[chosen]
            + [layer] * layers
            + [whole] * len(arrived)
            + [pl.BlockSpec(memory_space=pl.ANY)] * len(after),
            out_specs=out_specs,
        ),
        out_shape=out_shape,
        compiler_params=room,
        cost_estimate=cost_of(*[summed] * (3 + len(arrived))),
        name="shard_sum",
    )(shards, keep, *theirs, *arrived, *after)


def update_kernel(count, bound, scales_ref, squares_ref, *rest):
    states, grads, outs = (rest[:3], rest[3:6]), rest[6 : 6 + 2 * count], rest[6 + 2 * count :]
    step = pl.program_id(0)
    per = pl.num_programs(0) // (2 * count)
    factor = jnp.minimum(
        jnp.float32(1.0), bound / (jnp.sqrt(jnp.sum(squares_ref[...])) + jnp.float32(1e-06))
    )
    for index, grad_ref in enumerate(grads):

        @pl.when(step // per == index)
        def _(index=index, grad_ref=grad_ref):
            who = index // count
            new = adamw_update(
                *[ref[...] for ref in states[who]],
                grad_ref[...],
                factor,
                scales_ref[0],
                scales_ref[1],
            )
            for out_ref, value in zip(outs[3 * who : 3 * who + 3], new):
                out_ref[...] = value


def update(scales, squares, state, grads, old_copy, peer_grads, bound):
    layers, own, columns = state[0].shape
    width = grads[0].shape[-1]
    count = len(grads)
    size = block_of(width, 12288)
    per, blocks = width // size, columns // size
    shape = (layers, own, size)

    def part(first, many, row=0):
        return pl.BlockSpec(shape, lambda i: (row, 0, jnp.clip(i - first, 0, many - 1)))

    return pl.pallas_call(
        functools.partial(update_kernel, count, bound),
        grid=(2 * blocks,),
        in_specs=[
            pl.BlockSpec(memory_space=pltpu.SMEM),
            pl.BlockSpec(squares.shape, lambda i: (0, 0)),
        ]
        + [part(0, blocks)] * 3
        + [part(blocks, blocks, row) for row in range(3)]
        + [part(k * per, per) for k in range(2 * count)],
        out_specs=[part(0, blocks)] * 3 + [part(blocks, blocks)] * 3,
        out_shape=[jax.ShapeDtypeStruct((layers, own, columns), jnp.float32)] * 6,
        compiler_params=room,
        cost_estimate=cost_of(*[state[0]] * 14),
        name="update",
    )(scales, squares, *state, *[old_copy] * 3, *grads, *peer_grads)


def total_over(value, axis):
    peers = lax.axis_size(axis)
    if peers & (peers - 1):
        return lax.psum(value, axis)
    bit = 1
    while bit < peers:
        value = value + lax.ppermute(value, axis, [(i, i ^ bit) for i in range(peers)])
        bit *= 2
    return value


def local(acc_grads, activations, cotangent, params, first_moment, second_moment, step):
    _, layers, rows, columns = acc_grads.shape
    tokens = activations.shape[0]
    peers = lax.axis_size("dp")
    chips = peers // 2
    half = chips // 2
    order = [2 * z for z in range(half)] + [2 * z + 1 for z in reversed(range(half))]

    def hop(by):
        return [
            (2 * order[r] + core, 2 * order[(r + by) % chips] + core)
            for r in range(chips)
            for core in range(2)
        ]

    swap = [(i, i ^ 1) for i in range(peers)]
    onward = [(i, (i + 1) % peers) for i in range(peers)]

    index = lax.axis_index("dp")
    core, chip = index % 2, index // 2
    place = jnp.where(chip % 2 == 0, chip // 2, chips - 1 - chip // 2)
    hops = jnp.arange(half + 1, dtype=jnp.int32)
    tables = [
        jnp.concatenate([jnp.mod(place + by * hops, chips), core.reshape(1)]) for by in (1, -1)
    ]

    state = (params, first_moment, second_moment)
    old_copy = lax.ppermute(jnp.concatenate(state), "dp", onward)

    same = jnp.eye(layers, dtype=activations.dtype)
    inputs = activations.transpose(1, 2, 0)[:, :, :, None] * same[:, None, None, :]
    inputs = inputs.reshape(layers * rows, tokens * layers)

    width = columns // streams
    keep, theirs, sent, grads, peer_grads = ([None] * streams for _ in range(5))
    for k in range(streams):
        keep[k], *gives = make_terms(
            core.reshape(1), inputs, acc_grads, cotangent, order, k * width, width
        )
        theirs[k] = [lax.ppermute(give, "dp", swap) for give in gives]
    for k in range(streams):
        total = shard_sum(
            plain_kernel, tables[0], half, keep[k], theirs[k], after=() if k else [old_copy]
        )
        sent[k] = [None, None]
        sent[k][k % 2] = lax.ppermute(total, "dp", hop(-1 if k % 2 else 1))
    for away in range(half - 1, 0, -1):
        for k in range(streams):
            for way, by in enumerate((1, -1)):
                arrived = [] if sent[k][way] is None else [sent[k][way]]
                body = step_kernel if arrived else plain_kernel
                total = shard_sum(body, tables[way], away, keep[k], theirs[k], *arrived)
                sent[k][way] = lax.ppermute(total, "dp", hop(by))
    squares = None
    for k in range(streams):
        grads[k], part = shard_sum(last_kernel, tables[0], 0, keep[k], theirs[k], *sent[k])
        peer_grads[k] = lax.ppermute(grads[k], "dp", onward)
        squares = part if squares is None else squares + part

    squares = total_over(total_over(squares, "dp"), "mp")
    bound = float((layers * rows * columns * lax.axis_size("mp")) ** 0.5)
    count = step.astype(jnp.float32)
    scales = jnp.concatenate(
        [
            1.0 - jnp.power(jnp.float32(beta_one), count),
            1.0 - jnp.power(jnp.float32(beta_two), count),
        ]
    )
    return tuple(update(scales, squares, state, grads, old_copy, peer_grads, bound))


def solution(mesh):
    owned = P(None, "dp", "mp")
    return jax.shard_map(
        local,
        mesh=mesh,
        in_specs=(
            P("dp", None, None, "mp"),
            P("dp", None, None),
            P("dp", None, "mp"),
            owned,
            owned,
            owned,
            P(),
        ),
        out_specs=(owned,) * 6,
        check_vma=False,
    )
```

```python
import functools
import math

import jax
import jax.numpy as jnp
from jax import lax
from jax.experimental import pallas as pl
from jax.experimental.pallas import tpu as pltpu
from jax.sharding import PartitionSpec as P

beta_one = 0.9
beta_two = 0.95
learn_rate = 0.1
decay_rate = 0.1
epsilon = 1e-08

streams = 2
lanes = 128
room = pltpu.CompilerParams(vmem_limit_bytes=64*2**20)


def block_of(columns, most):
    best = lanes
    for size in range(lanes, min(columns, most) + 1, lanes):
        if columns % size == 0:
            best = size
    return best


def cost_of(*arrays):
    moved = sum(math.prod(a.shape) * jnp.dtype(a.dtype).itemsize for a in arrays)
    return pl.CostEstimate(flops=0, bytes_accessed=moved, transcendentals=0)


def adamw_update(weights, first, second, grad, factor, first_scale, second_scale):
    scaled = factor * grad
    first_new = beta_one * first + (1.0 - beta_one) * scaled
    second_new = beta_two * second + (1.0 - beta_two) * scaled * scaled
    first_hat = first_new / first_scale
    second_hat = second_new / second_scale
    weights_new = weights - learn_rate * (
        first_hat / (jnp.sqrt(second_hat) + epsilon) + decay_rate * weights
    )
    return (weights_new, first_new, second_new)


def terms_kernel(order, layers, core_ref, inputs_ref, earlier_ref, outgrad_ref, *rest):
    keep_ref, gives = rest[-1 - layers], rest[-layers:]
    core = core_ref[0]
    tokens, _, columns = outgrad_ref.shape
    rows = earlier_ref.shape[2]
    outgrad = outgrad_ref[...].reshape(tokens * layers, columns)
    product = jnp.dot(inputs_ref[...], outgrad, preferred_element_type=jnp.float32)
    chips = len(order)
    for layer in range(layers):
        total = earlier_ref[0, layer].astype(jnp.float32) + product[layer * rows : (layer + 1) * rows]
        term = total.astype(jnp.bfloat16).astype(jnp.float32)
        term = term.reshape(chips, 2, rows // (2 * chips), columns)
        for place, chip in enumerate(order):
            keep_ref[place, layer] = jnp.where(core == 0, term[chip, 0], term[chip, 1])
            gives[layer][place] = jnp.where(core == 0, term[chip, 1], term[chip, 0])


def make_terms(core, inputs, earlier, outgrad, order, start, width):
    _, layers, rows, _ = earlier.shape
    tokens = outgrad.shape[0]
    chips = len(order)
    own = rows // (2 * chips)
    size = block_of(width, 6144)
    first = start // size
    return pl.pallas_call(
        functools.partial(terms_kernel, order, layers),
        grid_spec=pltpu.PrefetchScalarGridSpec(
            num_scalar_prefetch=1,
            grid=(width // size,),
            in_specs=[
                pl.BlockSpec(inputs.shape, lambda i, core: (0, 0)),
                pl.BlockSpec((1, layers, rows, size), lambda i, core: (0, 0, 0, first + i)),
                pl.BlockSpec((tokens, layers, size), lambda i, core: (0, 0, first + i)),
            ],
            out_specs=[pl.BlockSpec((chips, layers, own, size), lambda i, core: (0, 0, 0, i))]
            + [pl.BlockSpec((chips, own, size), lambda i, core: (0, 0, i))] * layers,
        ),
        out_shape=[jax.ShapeDtypeStruct((chips, layers, own, width), jnp.float32)]
        + [jax.ShapeDtypeStruct((chips, own, width), jnp.float32)] * layers,
        compiler_params=room,
        cost_estimate=cost_of(
            jax.ShapeDtypeStruct((layers, rows + tokens, width), earlier.dtype),
            jax.ShapeDtypeStruct((layers, rows, width), jnp.float32),
        ),
        name="terms",
    )(core, inputs, earlier, outgrad)


def both_cores(keep_ref, theirs):
    return jnp.stack([keep_ref[0, layer] + theirs_ref[0] for layer, theirs_ref in enumerate(theirs)])


def plain_kernel(layers, shard_ref, keep_ref, *rest):
    theirs, out_ref = rest[:layers], rest[-1]
    out_ref[...] = both_cores(keep_ref, theirs)


def step_kernel(layers, shard_ref, keep_ref, *rest):
    theirs, arrived_ref, out_ref = rest[:layers], rest[layers], rest[-1]
    out_ref[...] = arrived_ref[...] + both_cores(keep_ref, theirs)


def last_kernel(layers, shard_ref, keep_ref, *rest):
    theirs, up_ref, down_ref = rest[:layers], rest[layers], rest[layers + 1]
    out_ref, squares_ref = rest[-2:]
    grad = (up_ref[...] + down_ref[...]) + both_cores(keep_ref, theirs)
    out_ref[...] = grad
    _, own, columns = grad.shape
    squares = jnp.sum((grad * grad).reshape(layers, own, columns // lanes, lanes), axis=(0, 2))

    @pl.when(pl.program_id(0) == 0)
    def _():
        squares_ref[...] = squares

    @pl.when(pl.program_id(0) > 0)
    def _():
        squares_ref[...] += squares


def shard_sum(body, shards, which, keep, theirs, *arrived, after=()):
    _, layers, own, width = keep.shape
    size = block_of(width, 6144)
    chosen = pl.BlockSpec((1, layers, own, size), lambda i, shards: (shards[which], 0, 0, i))
    layer = pl.BlockSpec((1, own, size), lambda i, shards: (shards[which], 0, i))
    whole = pl.BlockSpec((layers, own, size), lambda i, shards: (0, 0, i))
    summed = jax.ShapeDtypeStruct((layers, own, width), jnp.float32)
    out_shape, out_specs = summed, whole
    if body is last_kernel:
        out_shape = [summed, jax.ShapeDtypeStruct((own, lanes), jnp.float32)]
        out_specs = [whole, pl.BlockSpec((own, lanes), lambda i, shards: (0, 0))]
    return pl.pallas_call(
        functools.partial(body, layers),
        grid_spec=pltpu.PrefetchScalarGridSpec(
            num_scalar_prefetch=1,
            grid=(width // size,),
            in_specs=[chosen]
            + [layer] * layers
            + [whole] * len(arrived)
            + [pl.BlockSpec(memory_space=pl.ANY)] * len(after),
            out_specs=out_specs,
        ),
        out_shape=out_shape,
        compiler_params=room,
        cost_estimate=cost_of(*[summed] * (3 + len(arrived))),
        name="shard_sum",
    )(shards, keep, *theirs, *arrived, *after)


def update_kernel(count, bound, scales_ref, squares_ref, *rest):
    states, grads, outs = (rest[:3], rest[3:6]), rest[6 : 6 + 2 * count], rest[6 + 2 * count :]
    step = pl.program_id(0)
    per = pl.num_programs(0) // count
    factor = jnp.minimum(
        jnp.float32(1.0), bound / (jnp.sqrt(jnp.sum(squares_ref[...])) + jnp.float32(1e-06))
    )
    for index in range(count):

        @pl.when(step // per == index)
        def _(index=index):
            for who in range(2):
                new = adamw_update(
                    *[ref[...] for ref in states[who]],
                    grads[who * count + index][...],
                    factor,
                    scales_ref[0],
                    scales_ref[1],
                )
                for out_ref, value in zip(outs[3 * who : 3 * who + 3], new):
                    out_ref[...] = value


def update(scales, squares, state, grads, old_copy, peer_grads, bound):
    layers, own, columns = state[0].shape
    width = grads[0].shape[-1]
    count = len(grads)
    size = block_of(width, 12288)
    per, blocks = width // size, columns // size
    shape = (layers, own, size)

    def part(first, many, row=0):
        return pl.BlockSpec(shape, lambda i: (row, 0, jnp.clip(i - first, 0, many - 1)))

    return pl.pallas_call(
        functools.partial(update_kernel, count, bound),
        grid=(blocks,),
        in_specs=[
            pl.BlockSpec(memory_space=pltpu.SMEM),
            pl.BlockSpec(squares.shape, lambda i: (0, 0)),
        ]
        + [part(0, blocks)] * 3
        + [part(0, blocks, row) for row in range(3)]
        + [part(k * per, per) for k in range(count)] * 2,
        out_specs=[part(0, blocks)] * 6,
        out_shape=[jax.ShapeDtypeStruct((layers, own, columns), jnp.float32)] * 6,
        compiler_params=room,
        cost_estimate=cost_of(*[state[0]] * 14),
        name="update",
    )(scales, squares, *state, *[old_copy] * 3, *grads, *peer_grads)


def joined_kernel(*refs):
    *parts, out_ref = refs
    layers = parts[0].shape[0]
    for index, part_ref in enumerate(parts):
        out_ref[index * layers : (index + 1) * layers] = part_ref[...]


def joined(arrays):
    layers, own, columns = arrays[0].shape
    size = block_of(columns, 8192)
    return pl.pallas_call(
        joined_kernel,
        grid=(columns // size,),
        in_specs=[pl.BlockSpec((layers, own, size), lambda i: (0, 0, i))] * len(arrays),
        out_specs=pl.BlockSpec((len(arrays) * layers, own, size), lambda i: (0, 0, i)),
        out_shape=jax.ShapeDtypeStruct((len(arrays) * layers, own, columns), jnp.float32),
        compiler_params=room,
        cost_estimate=cost_of(*arrays, *arrays),
        name="joined",
    )(*arrays)


def total_over(value, axis):
    peers = lax.axis_size(axis)
    if peers & (peers - 1):
        return lax.psum(value, axis)
    bit = 1
    while bit < peers:
        value = value + lax.ppermute(value, axis, [(i, i ^ bit) for i in range(peers)])
        bit *= 2
    return value


def local(acc_grads, activations, cotangent, params, first_moment, second_moment, step):
    _, layers, rows, columns = acc_grads.shape
    tokens = activations.shape[0]
    peers = lax.axis_size("dp")
    chips = peers // 2
    half = chips // 2
    order = [2 * z for z in range(half)] + [2 * z + 1 for z in reversed(range(half))]

    def hop(by):
        return [
            (2 * order[r] + core, 2 * order[(r + by) % chips] + core)
            for r in range(chips)
            for core in range(2)
        ]

    swap = [(i, i ^ 1) for i in range(peers)]
    onward = [(i, (i + 1) % peers) for i in range(peers)]

    index = lax.axis_index("dp")
    core, chip = index % 2, index // 2
    place = jnp.where(chip % 2 == 0, chip // 2, chips - 1 - chip // 2)
    hops = jnp.arange(half + 1, dtype=jnp.int32)
    tables = [
        jnp.concatenate([jnp.mod(place + by * hops, chips), core.reshape(1)]) for by in (1, -1)
    ]

    state = (params, first_moment, second_moment)
    old_copy = lax.ppermute(joined(state), "dp", onward)

    same = jnp.eye(layers, dtype=activations.dtype)
    inputs = activations.transpose(1, 2, 0)[:, :, :, None] * same[:, None, None, :]
    inputs = inputs.reshape(layers * rows, tokens * layers)

    width = columns // streams
    keep, theirs, sent, grads, peer_grads = ([None] * streams for _ in range(5))
    for k in range(streams):
        keep[k], *gives = make_terms(
            core.reshape(1), inputs, acc_grads, cotangent, order, k * width, width
        )
        theirs[k] = [lax.ppermute(give, "dp", swap) for give in gives]
    for k in range(streams):
        total = shard_sum(
            plain_kernel, tables[0], half, keep[k], theirs[k]
        )
        sent[k] = [None, None]
        sent[k][k % 2] = lax.ppermute(total, "dp", hop(-1 if k % 2 else 1))
    waiting = [old_copy]
    for away in range(half - 1, 0, -1):
        for k in range(streams):
            for way, by in enumerate((1, -1)):
                arrived = [] if sent[k][way] is None else [sent[k][way]]
                body = step_kernel if arrived else plain_kernel
                after = []
                if arrived:
                    after, waiting = waiting, after
                total = shard_sum(
                    body, tables[way], away, keep[k], theirs[k], *arrived, after=after
                )
                sent[k][way] = lax.ppermute(total, "dp", hop(by))
    squares = None
    for k in range(streams):
        grads[k], part = shard_sum(last_kernel, tables[0], 0, keep[k], theirs[k], *sent[k])
        peer_grads[k] = lax.ppermute(grads[k], "dp", onward)
        squares = part if squares is None else squares + part

    squares = total_over(total_over(squares, "dp"), "mp")
    bound = float((layers * rows * columns * lax.axis_size("mp")) ** 0.5)
    count = step.astype(jnp.float32)
    scales = jnp.concatenate(
        [
            1.0 - jnp.power(jnp.float32(beta_one), count),
            1.0 - jnp.power(jnp.float32(beta_two), count),
        ]
    )
    return tuple(update(scales, squares, state, grads, old_copy, peer_grads, bound))


def solution(mesh):
    owned = P(None, "dp", "mp")
    return jax.shard_map(
        local,
        mesh=mesh,
        in_specs=(
            P("dp", None, None, "mp"),
            P("dp", None, None),
            P("dp", None, "mp"),
            owned,
            owned,
            owned,
            P(),
        ),
        out_specs=(owned,) * 6,
        check_vma=False,
    )
```

```python
import functools
import math

import jax
import jax.numpy as jnp
from jax import lax
from jax.experimental import pallas as pl
from jax.experimental.pallas import tpu as pltpu
from jax.sharding import PartitionSpec as P

beta_one = 0.9
beta_two = 0.95
learn_rate = 0.1
decay_rate = 0.1
epsilon = 1e-08

streams = 2
lanes = 128
room = pltpu.CompilerParams(vmem_limit_bytes=64*2**20)


def block_of(columns, most):
    best = lanes
    for size in range(lanes, min(columns, most) + 1, lanes):
        if columns % size == 0:
            best = size
    return best


def cost_of(*arrays):
    moved = sum(math.prod(a.shape) * jnp.dtype(a.dtype).itemsize for a in arrays)
    return pl.CostEstimate(flops=0, bytes_accessed=moved, transcendentals=0)


def adamw_update(weights, first, second, grad, factor, first_scale, second_scale):
    scaled = factor * grad
    first_new = beta_one * first + (1.0 - beta_one) * scaled
    second_new = beta_two * second + (1.0 - beta_two) * scaled * scaled
    first_hat = first_new / first_scale
    second_hat = second_new / second_scale
    weights_new = weights - learn_rate * (
        first_hat / (jnp.sqrt(second_hat) + epsilon) + decay_rate * weights
    )
    return (weights_new, first_new, second_new)


def terms_kernel(order, layers, core_ref, inputs_ref, earlier_ref, outgrad_ref, *rest):
    keep_ref, gives = rest[-1 - layers], rest[-layers:]
    core = core_ref[0]
    tokens, _, columns = outgrad_ref.shape
    rows = earlier_ref.shape[2]
    outgrad = outgrad_ref[...].reshape(tokens * layers, columns)
    product = jnp.dot(inputs_ref[...], outgrad, preferred_element_type=jnp.float32)
    chips = len(order)
    for layer in range(layers):
        total = earlier_ref[0, layer].astype(jnp.float32) + product[layer * rows : (layer + 1) * rows]
        term = total.astype(jnp.bfloat16).astype(jnp.float32)
        term = term.reshape(chips, 2, rows // (2 * chips), columns)
        for place, chip in enumerate(order):
            keep_ref[place, layer] = jnp.where(core == 0, term[chip, 0], term[chip, 1])
            gives[layer][place] = jnp.where(core == 0, term[chip, 1], term[chip, 0])


def make_terms(core, inputs, earlier, outgrad, order, start, width):
    _, layers, rows, _ = earlier.shape
    tokens = outgrad.shape[0]
    chips = len(order)
    own = rows // (2 * chips)
    size = block_of(width, 6144)
    first = start // size
    return pl.pallas_call(
        functools.partial(terms_kernel, order, layers),
        grid_spec=pltpu.PrefetchScalarGridSpec(
            num_scalar_prefetch=1,
            grid=(width // size,),
            in_specs=[
                pl.BlockSpec(inputs.shape, lambda i, core: (0, 0)),
                pl.BlockSpec((1, layers, rows, size), lambda i, core: (0, 0, 0, first + i)),
                pl.BlockSpec((tokens, layers, size), lambda i, core: (0, 0, first + i)),
            ],
            out_specs=[pl.BlockSpec((chips, layers, own, size), lambda i, core: (0, 0, 0, i))]
            + [pl.BlockSpec((chips, own, size), lambda i, core: (0, 0, i))] * layers,
        ),
        out_shape=[jax.ShapeDtypeStruct((chips, layers, own, width), jnp.float32)]
        + [jax.ShapeDtypeStruct((chips, own, width), jnp.float32)] * layers,
        compiler_params=room,
        cost_estimate=cost_of(
            jax.ShapeDtypeStruct((layers, rows + tokens, width), earlier.dtype),
            jax.ShapeDtypeStruct((layers, rows, width), jnp.float32),
        ),
        name="terms",
    )(core, inputs, earlier, outgrad)


def both_cores(keep_ref, theirs):
    return jnp.stack([keep_ref[0, layer] + theirs_ref[0] for layer, theirs_ref in enumerate(theirs)])


def plain_kernel(layers, shard_ref, keep_ref, *rest):
    theirs, out_ref = rest[:layers], rest[-1]
    out_ref[...] = both_cores(keep_ref, theirs)


def step_kernel(layers, shard_ref, keep_ref, *rest):
    theirs, arrived_ref, out_ref = rest[:layers], rest[layers], rest[-1]
    out_ref[...] = arrived_ref[...] + both_cores(keep_ref, theirs)


def last_kernel(layers, shard_ref, keep_ref, *rest):
    theirs, up_ref, down_ref = rest[:layers], rest[layers], rest[layers + 1]
    out_ref, squares_ref = rest[-2:]
    grad = (up_ref[...] + down_ref[...]) + both_cores(keep_ref, theirs)
    out_ref[...] = grad
    _, own, columns = grad.shape
    squares = jnp.sum((grad * grad).reshape(layers, own, columns // lanes, lanes), axis=(0, 2))

    @pl.when(pl.program_id(0) == 0)
    def _():
        squares_ref[...] = squares

    @pl.when(pl.program_id(0) > 0)
    def _():
        squares_ref[...] += squares


def shard_sum(body, shards, which, keep, theirs, *arrived, after=()):
    _, layers, own, width = keep.shape
    size = block_of(width, 6144)
    chosen = pl.BlockSpec((1, layers, own, size), lambda i, shards: (shards[which], 0, 0, i))
    layer = pl.BlockSpec((1, own, size), lambda i, shards: (shards[which], 0, i))
    whole = pl.BlockSpec((layers, own, size), lambda i, shards: (0, 0, i))
    summed = jax.ShapeDtypeStruct((layers, own, width), jnp.float32)
    out_shape, out_specs = summed, whole
    if body is last_kernel:
        out_shape = [summed, jax.ShapeDtypeStruct((own, lanes), jnp.float32)]
        out_specs = [whole, pl.BlockSpec((own, lanes), lambda i, shards: (0, 0))]
    return pl.pallas_call(
        functools.partial(body, layers),
        grid_spec=pltpu.PrefetchScalarGridSpec(
            num_scalar_prefetch=1,
            grid=(width // size,),
            in_specs=[chosen]
            + [layer] * layers
            + [whole] * len(arrived)
            + [pl.BlockSpec(memory_space=pl.ANY)] * len(after),
            out_specs=out_specs,
        ),
        out_shape=out_shape,
        compiler_params=room,
        cost_estimate=cost_of(*[summed] * (3 + len(arrived))),
        name="shard_sum",
    )(shards, keep, *theirs, *arrived, *after)


def update_kernel(count, bound, scales_ref, squares_ref, *rest):
    states, grads, outs = (rest[:3], rest[3:6]), rest[6 : 6 + 2 * count], rest[6 + 2 * count :]
    step = pl.program_id(0)
    per = pl.num_programs(0) // count
    factor = jnp.minimum(
        jnp.float32(1.0), bound / (jnp.sqrt(jnp.sum(squares_ref[...])) + jnp.float32(1e-06))
    )
    for index in range(count):

        @pl.when(step // per == index)
        def _(index=index):
            for who in range(2):
                new = adamw_update(
                    *[ref[...] for ref in states[who]],
                    grads[who * count + index][...],
                    factor,
                    scales_ref[0],
                    scales_ref[1],
                )
                for out_ref, value in zip(outs[3 * who : 3 * who + 3], new):
                    out_ref[...] = value


def update(scales, squares, state, grads, old_copy, peer_grads, bound):
    layers, own, columns = state[0].shape
    width = grads[0].shape[-1]
    count = len(grads)
    size = block_of(width, 12288)
    per, blocks = width // size, columns // size
    shape = (layers, own, size)

    def part(first, many, row=0):
        return pl.BlockSpec(shape, lambda i: (row, 0, jnp.clip(i - first, 0, many - 1)))

    return pl.pallas_call(
        functools.partial(update_kernel, count, bound),
        grid=(blocks,),
        in_specs=[
            pl.BlockSpec(memory_space=pltpu.SMEM),
            pl.BlockSpec(squares.shape, lambda i: (0, 0)),
        ]
        + [part(0, blocks)] * 3
        + [part(0, blocks, row) for row in range(3)]
        + [part(k * per, per) for k in range(count)] * 2,
        out_specs=[part(0, blocks)] * 6,
        out_shape=[jax.ShapeDtypeStruct((layers, own, columns), jnp.float32)] * 6,
        compiler_params=room,
        cost_estimate=cost_of(*[state[0]] * 14),
        name="update",
    )(scales, squares, *state, *[old_copy] * 3, *grads, *peer_grads)


def joined_kernel(*refs):
    *parts, out_ref = refs
    layers = parts[0].shape[0]
    for index, part_ref in enumerate(parts):
        out_ref[index * layers : (index + 1) * layers] = part_ref[...]


def joined(arrays):
    layers, own, columns = arrays[0].shape
    size = block_of(columns, 12288)
    return pl.pallas_call(
        joined_kernel,
        grid=(columns // size,),
        in_specs=[pl.BlockSpec((layers, own, size), lambda i: (0, 0, i))] * len(arrays),
        out_specs=pl.BlockSpec((len(arrays) * layers, own, size), lambda i: (0, 0, i)),
        out_shape=jax.ShapeDtypeStruct((len(arrays) * layers, own, columns), jnp.float32),
        compiler_params=room,
        cost_estimate=cost_of(*arrays, *arrays),
        name="joined",
    )(*arrays)


def total_of(value, later):
    peers, groups = lax.axis_size("dp"), lax.axis_size("mp")
    if peers & (peers - 1) or groups & (groups - 1) or peers < 4:
        return lax.psum(value, ("dp", "mp")), later

    def exchanged(value, axis, members, bit):
        return value + lax.ppermute(value, axis, [(i, i ^ bit) for i in members])

    value = exchanged(value, "dp", range(peers), 1)
    value = exchanged(value, "dp", range(peers), 2)
    value, later = lax.optimization_barrier((value, later))
    first = [i for i in range(peers) if not i & 2]
    bit = 4
    while bit < peers:
        value = exchanged(value, "dp", first, bit)
        bit *= 2
    bit = 1
    while bit < groups:
        value = exchanged(value, "mp", range(groups), bit)
        bit *= 2
    passed = lax.ppermute(value, "dp", [(i, i | 2) for i in first])
    return jnp.where(lax.axis_index("dp") & 2 == 0, value, passed), later


def local(acc_grads, activations, cotangent, params, first_moment, second_moment, step):
    _, layers, rows, columns = acc_grads.shape
    tokens = activations.shape[0]
    peers = lax.axis_size("dp")
    chips = peers // 2
    half = chips // 2
    order = [2 * z for z in range(half)] + [2 * z + 1 for z in reversed(range(half))]

    def hop(by):
        return [
            (2 * order[r] + core, 2 * order[(r + by) % chips] + core)
            for r in range(chips)
            for core in range(2)
        ]

    swap = [(i, i ^ 1) for i in range(peers)]
    onward = [(i, (i + 1) % peers) for i in range(peers)]

    index = lax.axis_index("dp")
    core, chip = index % 2, index // 2
    place = jnp.where(chip % 2 == 0, chip // 2, chips - 1 - chip // 2)
    hops = jnp.arange(half + 1, dtype=jnp.int32)
    tables = [
        jnp.concatenate([jnp.mod(place + by * hops, chips), core.reshape(1)]) for by in (1, -1)
    ]

    state = (params, first_moment, second_moment)
    old_copy = lax.ppermute(joined(state), "dp", onward)

    same = jnp.eye(layers, dtype=activations.dtype)
    inputs = activations.transpose(1, 2, 0)[:, :, :, None] * same[:, None, None, :]
    inputs = inputs.reshape(layers * rows, tokens * layers)

    width = columns // streams
    keep, theirs, sent, grads, peer_grads = ([None] * streams for _ in range(5))
    for k in range(streams):
        keep[k], *gives = make_terms(
            core.reshape(1), inputs, acc_grads, cotangent, order, k * width, width
        )
        theirs[k] = [lax.ppermute(give, "dp", swap) for give in gives]
    for k in range(streams):
        total = shard_sum(
            plain_kernel, tables[0], half, keep[k], theirs[k]
        )
        sent[k] = [None, None]
        sent[k][k % 2] = lax.ppermute(total, "dp", hop(-1 if k % 2 else 1))
    waiting = [old_copy]
    for away in range(half - 1, 0, -1):
        for k in range(streams):
            for way, by in enumerate((1, -1)):
                arrived = [] if sent[k][way] is None else [sent[k][way]]
                body = step_kernel if arrived else plain_kernel
                after = []
                if arrived:
                    after, waiting = waiting, after
                total = shard_sum(
                    body, tables[way], away, keep[k], theirs[k], *arrived, after=after
                )
                sent[k][way] = lax.ppermute(total, "dp", hop(by))
    squares = None
    for k in range(streams):
        grads[k], part = shard_sum(last_kernel, tables[0], 0, keep[k], theirs[k], *sent[k])
        if k:
            peer_grads[k] = lax.ppermute(grads[k], "dp", onward)
        squares = part if squares is None else squares + part

    squares, waiting = total_of(squares, grads[0])
    peer_grads[0] = lax.ppermute(waiting, "dp", onward)
    bound = float((layers * rows * columns * lax.axis_size("mp")) ** 0.5)
    count = step.astype(jnp.float32)
    scales = jnp.concatenate(
        [
            1.0 - jnp.power(jnp.float32(beta_one), count),
            1.0 - jnp.power(jnp.float32(beta_two), count),
        ]
    )
    return tuple(update(scales, squares, state, grads, old_copy, peer_grads, bound))


def solution(mesh):
    owned = P(None, "dp", "mp")
    return jax.shard_map(
        local,
        mesh=mesh,
        in_specs=(
            P("dp", None, None, "mp"),
            P("dp", None, None),
            P("dp", None, "mp"),
            owned,
            owned,
            owned,
            P(),
        ),
        out_specs=(owned,) * 6,
        check_vma=False,
    )
```

```python
import functools
import math

import jax
import jax.numpy as jnp
from jax import lax
from jax.experimental import pallas as pl
from jax.experimental.pallas import tpu as pltpu
from jax.sharding import PartitionSpec as P

beta_one = 0.9
beta_two = 0.95
learn_rate = 0.1
decay_rate = 0.1
epsilon = 1e-08

streams = 2
lanes = 128
room = pltpu.CompilerParams(vmem_limit_bytes=64*2**20)


def block_of(columns, most):
    best = lanes
    for size in range(lanes, min(columns, most) + 1, lanes):
        if columns % size == 0:
            best = size
    return best


def cost_of(*arrays):
    moved = sum(math.prod(a.shape) * jnp.dtype(a.dtype).itemsize for a in arrays)
    return pl.CostEstimate(flops=0, bytes_accessed=moved, transcendentals=0)


def adamw_update(weights, first, second, grad, factor, first_scale, second_scale):
    scaled = factor * grad
    first_new = beta_one * first + (1.0 - beta_one) * scaled
    second_new = beta_two * second + (1.0 - beta_two) * scaled * scaled
    first_hat = first_new / first_scale
    second_hat = second_new / second_scale
    weights_new = weights - learn_rate * (
        first_hat / (jnp.sqrt(second_hat) + epsilon) + decay_rate * weights
    )
    return (weights_new, first_new, second_new)


def terms_kernel(order, layers, core_ref, inputs_ref, earlier_ref, outgrad_ref, *rest):
    keep_ref, gives = rest[-1 - layers], rest[-layers:]
    core = core_ref[0]
    tokens, _, columns = outgrad_ref.shape
    rows = earlier_ref.shape[2]
    outgrad = outgrad_ref[...].reshape(tokens * layers, columns)
    product = jnp.dot(inputs_ref[...], outgrad, preferred_element_type=jnp.float32)
    chips = len(order)
    for layer in range(layers):
        total = earlier_ref[0, layer].astype(jnp.float32) + product[layer * rows : (layer + 1) * rows]
        term = total.astype(jnp.bfloat16).astype(jnp.float32)
        term = term.reshape(chips, 2, rows // (2 * chips), columns)
        for place, chip in enumerate(order):
            keep_ref[place, layer] = jnp.where(core == 0, term[chip, 0], term[chip, 1])
            gives[layer][place] = jnp.where(core == 0, term[chip, 1], term[chip, 0])


def make_terms(core, inputs, earlier, outgrad, order, start, width):
    _, layers, rows, _ = earlier.shape
    tokens = outgrad.shape[0]
    chips = len(order)
    own = rows // (2 * chips)
    size = block_of(width, 6144)
    first = start // size
    return pl.pallas_call(
        functools.partial(terms_kernel, order, layers),
        grid_spec=pltpu.PrefetchScalarGridSpec(
            num_scalar_prefetch=1,
            grid=(width // size,),
            in_specs=[
                pl.BlockSpec(inputs.shape, lambda i, core: (0, 0)),
                pl.BlockSpec((1, layers, rows, size), lambda i, core: (0, 0, 0, first + i)),
                pl.BlockSpec((tokens, layers, size), lambda i, core: (0, 0, first + i)),
            ],
            out_specs=[pl.BlockSpec((chips, layers, own, size), lambda i, core: (0, 0, 0, i))]
            + [pl.BlockSpec((chips, own, size), lambda i, core: (0, 0, i))] * layers,
        ),
        out_shape=[jax.ShapeDtypeStruct((chips, layers, own, width), jnp.float32)]
        + [jax.ShapeDtypeStruct((chips, own, width), jnp.float32)] * layers,
        compiler_params=room,
        cost_estimate=cost_of(
            jax.ShapeDtypeStruct((layers, rows + tokens, width), earlier.dtype),
            jax.ShapeDtypeStruct((layers, rows, width), jnp.float32),
        ),
        name="terms",
    )(core, inputs, earlier, outgrad)


def both_cores(keep_ref, theirs):
    return jnp.stack([keep_ref[0, layer] + theirs_ref[0] for layer, theirs_ref in enumerate(theirs)])


def plain_kernel(layers, shard_ref, keep_ref, *rest):
    theirs, out_ref = rest[:layers], rest[-1]
    out_ref[...] = both_cores(keep_ref, theirs)


def step_kernel(layers, shard_ref, keep_ref, *rest):
    theirs, arrived_ref, out_ref = rest[:layers], rest[layers], rest[-1]
    out_ref[...] = arrived_ref[...] + both_cores(keep_ref, theirs)


def last_kernel(streams, layers, shard_ref, *refs):
    *refs, squares_ref = refs
    refs, outs = refs[:-streams], refs[-streams:]
    each = layers + 3
    step = pl.program_id(0)
    per = pl.num_programs(0) // streams

    @pl.when(step == 0)
    def _():
        squares_ref[...] = jnp.zeros_like(squares_ref)

    for k in range(streams):

        @pl.when(step // per == k)
        def _(k=k):
            keep_ref, *theirs, up_ref, down_ref = refs[k * each : (k + 1) * each]
            grad = (up_ref[...] + down_ref[...]) + both_cores(keep_ref, theirs)
            outs[k][...] = grad
            _, own, columns = grad.shape
            squares = (grad * grad).reshape(layers, own, columns // lanes, lanes)
            squares_ref[...] += jnp.sum(squares, axis=(0, 2))


def last_sums(shards, keep, theirs, sent):
    streams = len(keep)
    _, layers, own, width = keep[0].shape
    size = block_of(width, 6144)
    per = width // size
    operands, specs, outs = [], [], []
    for k in range(streams):
        place = lambda i, k=k: jnp.clip(i - k * per, 0, per - 1)
        operands += [keep[k], *theirs[k], *sent[k]]
        specs += [pl.BlockSpec((1, layers, own, size), lambda i, s, at=place: (s[0], 0, 0, at(i)))]
        specs += [pl.BlockSpec((1, own, size), lambda i, s, at=place: (s[0], 0, at(i)))] * layers
        outs += [pl.BlockSpec((layers, own, size), lambda i, s, at=place: (0, 0, at(i)))]
        specs += outs[-1:] * 2
    summed = jax.ShapeDtypeStruct((layers, own, width), jnp.float32)
    *grads, squares = pl.pallas_call(
        functools.partial(last_kernel, streams, layers),
        grid_spec=pltpu.PrefetchScalarGridSpec(
            num_scalar_prefetch=1,
            grid=(streams * per,),
            in_specs=specs,
            out_specs=outs + [pl.BlockSpec((own, lanes), lambda i, s: (0, 0))],
        ),
        out_shape=[summed] * streams + [jax.ShapeDtypeStruct((own, lanes), jnp.float32)],
        compiler_params=room,
        cost_estimate=cost_of(*[summed] * (5 * streams)),
        name="last_sums",
    )(shards, *operands)
    return grads, squares


def shard_sum(body, shards, which, keep, theirs, *arrived, after=()):
    _, layers, own, width = keep.shape
    size = block_of(width, 6144)
    chosen = pl.BlockSpec((1, layers, own, size), lambda i, shards: (shards[which], 0, 0, i))
    layer = pl.BlockSpec((1, own, size), lambda i, shards: (shards[which], 0, i))
    whole = pl.BlockSpec((layers, own, size), lambda i, shards: (0, 0, i))
    summed = jax.ShapeDtypeStruct((layers, own, width), jnp.float32)
    return pl.pallas_call(
        functools.partial(body, layers),
        grid_spec=pltpu.PrefetchScalarGridSpec(
            num_scalar_prefetch=1,
            grid=(width // size,),
            in_specs=[chosen]
            + [layer] * layers
            + [whole] * len(arrived)
            + [pl.BlockSpec(memory_space=pl.ANY)] * len(after),
            out_specs=whole,
        ),
        out_shape=summed,
        compiler_params=room,
        cost_estimate=cost_of(*[summed] * (3 + len(arrived))),
        name="shard_sum",
    )(shards, keep, *theirs, *arrived, *after)


def update_kernel(count, bound, scales_ref, squares_ref, *rest):
    states, grads, outs = (rest[:3], rest[3:6]), rest[6 : 6 + 2 * count], rest[6 + 2 * count :]
    step = pl.program_id(0)
    per = pl.num_programs(0) // count
    factor = jnp.minimum(
        jnp.float32(1.0), bound / (jnp.sqrt(jnp.sum(squares_ref[...])) + jnp.float32(1e-06))
    )
    for index in range(count):

        @pl.when(step // per == index)
        def _(index=index):
            for who in range(2):
                new = adamw_update(
                    *[ref[...] for ref in states[who]],
                    grads[who * count + index][...],
                    factor,
                    scales_ref[0],
                    scales_ref[1],
                )
                for out_ref, value in zip(outs[3 * who : 3 * who + 3], new):
                    out_ref[...] = value


def update(scales, squares, state, grads, old_copy, peer_grads, bound):
    layers, own, columns = state[0].shape
    width = grads[0].shape[-1]
    count = len(grads)
    size = block_of(width, 12288)
    per, blocks = width // size, columns // size
    shape = (layers, own, size)

    def part(first, many, row=0):
        return pl.BlockSpec(shape, lambda i: (row, 0, jnp.clip(i - first, 0, many - 1)))

    return pl.pallas_call(
        functools.partial(update_kernel, count, bound),
        grid=(blocks,),
        in_specs=[
            pl.BlockSpec(memory_space=pltpu.SMEM),
            pl.BlockSpec(squares.shape, lambda i: (0, 0)),
        ]
        + [part(0, blocks)] * 3
        + [part(0, blocks, row) for row in range(3)]
        + [part(k * per, per) for k in range(count)] * 2,
        out_specs=[part(0, blocks)] * 6,
        out_shape=[jax.ShapeDtypeStruct((layers, own, columns), jnp.float32)] * 6,
        compiler_params=room,
        cost_estimate=cost_of(*[state[0]] * 14),
        name="update",
    )(scales, squares, *state, *[old_copy] * 3, *grads, *peer_grads)


def joined_kernel(*refs):
    *parts, out_ref = refs
    layers = parts[0].shape[0]
    for index, part_ref in enumerate(parts):
        out_ref[index * layers : (index + 1) * layers] = part_ref[...]


def joined(arrays):
    layers, own, columns = arrays[0].shape
    size = block_of(columns, 12288)
    return pl.pallas_call(
        joined_kernel,
        grid=(columns // size,),
        in_specs=[pl.BlockSpec((layers, own, size), lambda i: (0, 0, i))] * len(arrays),
        out_specs=pl.BlockSpec((len(arrays) * layers, own, size), lambda i: (0, 0, i)),
        out_shape=jax.ShapeDtypeStruct((len(arrays) * layers, own, columns), jnp.float32),
        compiler_params=room,
        cost_estimate=cost_of(*arrays, *arrays),
        name="joined",
    )(*arrays)


def total_of(value, later, last):
    peers, groups = lax.axis_size("dp"), lax.axis_size("mp")
    if peers & (peers - 1) or groups & (groups - 1) or peers < 4:
        return lax.psum(value, ("dp", "mp")), later, last

    def exchanged(value, axis, members, *bits):
        others = [lax.ppermute(value, axis, [(i, i ^ bit) for i in members]) for bit in bits]
        return sum(others, value)

    value = exchanged(value, "dp", range(peers), 1)
    value, later = lax.optimization_barrier((value, later))
    value = exchanged(value, "dp", range(peers), 2)
    value, last = lax.optimization_barrier((value, last))
    first = [i for i in range(peers) if not i & 2]
    bit = 4
    while bit < peers:
        if 2 * bit < peers:
            value = exchanged(value, "dp", first, bit, 2 * bit, 3 * bit)
        else:
            value = exchanged(value, "dp", first, bit)
        bit *= 4
    bit = 1
    while bit < groups:
        value = exchanged(value, "mp", range(groups), bit)
        bit *= 2
    passed = lax.ppermute(value, "dp", [(i, i | 2) for i in first])
    return jnp.where(lax.axis_index("dp") & 2 == 0, value, passed), later, last


def local(acc_grads, activations, cotangent, params, first_moment, second_moment, step):
    _, layers, rows, columns = acc_grads.shape
    tokens = activations.shape[0]
    peers = lax.axis_size("dp")
    chips = peers // 2
    half = chips // 2
    order = [2 * z for z in range(half)] + [2 * z + 1 for z in reversed(range(half))]

    def hop(by):
        return [
            (2 * order[r] + core, 2 * order[(r + by) % chips] + core)
            for r in range(chips)
            for core in range(2)
        ]

    swap = [(i, i ^ 1) for i in range(peers)]
    onward = [(i, (i + 1) % peers) for i in range(peers)]

    index = lax.axis_index("dp")
    core, chip = index % 2, index // 2
    place = jnp.where(chip % 2 == 0, chip // 2, chips - 1 - chip // 2)
    hops = jnp.arange(half + 1, dtype=jnp.int32)
    tables = [
        jnp.concatenate([jnp.mod(place + by * hops, chips), core.reshape(1)]) for by in (1, -1)
    ]

    state = (params, first_moment, second_moment)
    old_copy = lax.ppermute(joined(state), "dp", onward)

    same = jnp.eye(layers, dtype=activations.dtype)
    inputs = activations.transpose(1, 2, 0)[:, :, :, None] * same[:, None, None, :]
    inputs = inputs.reshape(layers * rows, tokens * layers)

    width = columns // streams
    keep, theirs, sent = ([None] * streams for _ in range(3))
    for k in range(streams):
        keep[k], *gives = make_terms(
            core.reshape(1), inputs, acc_grads, cotangent, order, k * width, width
        )
        theirs[k] = [lax.ppermute(give, "dp", swap) for give in gives]
    for k in range(streams):
        total = shard_sum(
            plain_kernel, tables[0], half, keep[k], theirs[k]
        )
        sent[k] = [None, None]
        sent[k][k % 2] = lax.ppermute(total, "dp", hop(-1 if k % 2 else 1))
    waiting = [old_copy]
    for away in range(half - 1, 0, -1):
        for k in range(streams):
            for way, by in enumerate((1, -1)):
                arrived = [] if sent[k][way] is None else [sent[k][way]]
                body = step_kernel if arrived else plain_kernel
                after = []
                if arrived:
                    after, waiting = waiting, after
                total = shard_sum(
                    body, tables[way], away, keep[k], theirs[k], *arrived, after=after
                )
                sent[k][way] = lax.ppermute(total, "dp", hop(by))
    grads, squares = last_sums(tables[0], keep, theirs, sent)
    squares, *waiting = total_of(squares, grads[1:], grads[:1])
    peer_grads = [lax.ppermute(value, "dp", onward) for value in waiting[1] + waiting[0]]
    bound = float((layers * rows * columns * lax.axis_size("mp")) ** 0.5)
    count = step.astype(jnp.float32)
    scales = jnp.concatenate(
        [
            1.0 - jnp.power(jnp.float32(beta_one), count),
            1.0 - jnp.power(jnp.float32(beta_two), count),
        ]
    )
    return tuple(update(scales, squares, state, grads, old_copy, peer_grads, bound))


def solution(mesh):
    owned = P(None, "dp", "mp")
    return jax.shard_map(
        local,
        mesh=mesh,
        in_specs=(
            P("dp", None, None, "mp"),
            P("dp", None, None),
            P("dp", None, "mp"),
            owned,
            owned,
            owned,
            P(),
        ),
        out_specs=(owned,) * 6,
        check_vma=False,
    )
```

```python
import functools
import math

import jax
import jax.numpy as jnp
from jax import lax
from jax.experimental import pallas as pl
from jax.experimental.pallas import tpu as pltpu
from jax.sharding import PartitionSpec as P

beta_one = 0.9
beta_two = 0.95
learn_rate = 0.1
decay_rate = 0.1
epsilon = 1e-08

streams = 2
lanes = 128
room = pltpu.CompilerParams(vmem_limit_bytes=64*2**20)


def block_of(columns, most):
    best = lanes
    for size in range(lanes, min(columns, most) + 1, lanes):
        if columns % size == 0:
            best = size
    return best


def cost_of(*arrays):
    moved = sum(math.prod(a.shape) * jnp.dtype(a.dtype).itemsize for a in arrays)
    return pl.CostEstimate(flops=0, bytes_accessed=moved, transcendentals=0)


def adamw_update(weights, first, second, grad, factor, first_scale, second_scale):
    scaled = factor * grad
    first_new = beta_one * first + (1.0 - beta_one) * scaled
    second_new = beta_two * second + (1.0 - beta_two) * scaled * scaled
    first_hat = first_new / first_scale
    second_hat = second_new / second_scale
    weights_new = weights - learn_rate * (
        first_hat / (jnp.sqrt(second_hat) + epsilon) + decay_rate * weights
    )
    return (weights_new, first_new, second_new)


def terms_kernel(order, layers, core_ref, inputs_ref, earlier_ref, outgrad_ref, *rest):
    keep_ref, gives = rest[-1 - layers], rest[-layers:]
    core = core_ref[0]
    tokens, _, columns = outgrad_ref.shape
    rows = earlier_ref.shape[2]
    outgrad = outgrad_ref[...].reshape(tokens * layers, columns)
    product = jnp.dot(inputs_ref[...], outgrad, preferred_element_type=jnp.float32)
    chips = len(order)
    for layer in range(layers):
        total = earlier_ref[0, layer].astype(jnp.float32) + product[layer * rows : (layer + 1) * rows]
        term = total.astype(jnp.bfloat16).astype(jnp.float32)
        term = term.reshape(chips, 2, rows // (2 * chips), columns)
        for place, chip in enumerate(order):
            keep_ref[place, layer] = jnp.where(core == 0, term[chip, 0], term[chip, 1])
            gives[layer][place] = jnp.where(core == 0, term[chip, 1], term[chip, 0])


def make_terms(core, inputs, earlier, outgrad, order, start, width):
    _, layers, rows, _ = earlier.shape
    tokens = outgrad.shape[0]
    chips = len(order)
    own = rows // (2 * chips)
    size = block_of(width, 6144)
    first = start // size
    return pl.pallas_call(
        functools.partial(terms_kernel, order, layers),
        grid_spec=pltpu.PrefetchScalarGridSpec(
            num_scalar_prefetch=1,
            grid=(width // size,),
            in_specs=[
                pl.BlockSpec(inputs.shape, lambda i, core: (0, 0)),
                pl.BlockSpec((1, layers, rows, size), lambda i, core: (0, 0, 0, first + i)),
                pl.BlockSpec((tokens, layers, size), lambda i, core: (0, 0, first + i)),
            ],
            out_specs=[pl.BlockSpec((chips, layers, own, size), lambda i, core: (0, 0, 0, i))]
            + [pl.BlockSpec((chips, own, size), lambda i, core: (0, 0, i))] * layers,
        ),
        out_shape=[jax.ShapeDtypeStruct((chips, layers, own, width), jnp.float32)]
        + [jax.ShapeDtypeStruct((chips, own, width), jnp.float32)] * layers,
        compiler_params=room,
        cost_estimate=cost_of(
            jax.ShapeDtypeStruct((layers, rows + tokens, width), earlier.dtype),
            jax.ShapeDtypeStruct((layers, rows, width), jnp.float32),
        ),
        name="terms",
    )(core, inputs, earlier, outgrad)


def both_cores(keep_ref, theirs):
    return jnp.stack([keep_ref[0, layer] + theirs_ref[0] for layer, theirs_ref in enumerate(theirs)])


def plain_kernel(layers, shard_ref, keep_ref, *rest):
    theirs, out_ref = rest[:layers], rest[-1]
    out_ref[...] = both_cores(keep_ref, theirs)


def step_kernel(layers, shard_ref, keep_ref, *rest):
    theirs, arrived_ref, out_ref = rest[:layers], rest[layers], rest[-1]
    out_ref[...] = arrived_ref[...] + both_cores(keep_ref, theirs)


def last_kernel(streams, *refs):
    *refs, squares_ref = refs
    refs, outs = refs[:-streams], refs[-streams:]
    step = pl.program_id(0)
    per = pl.num_programs(0) // streams

    @pl.when(step == 0)
    def _():
        squares_ref[...] = jnp.zeros_like(squares_ref)

    for k in range(streams):

        @pl.when(step // per == k)
        def _(k=k):
            own_ref, up_ref, down_ref = refs[3 * k : 3 * k + 3]
            grad = (up_ref[...] + down_ref[...]) + own_ref[...]
            outs[k][...] = grad
            layers, own, columns = grad.shape
            squares = (grad * grad).reshape(layers, own, columns // lanes, lanes)
            squares_ref[...] += jnp.sum(squares, axis=(0, 2))


def last_sums(ours, sent):
    streams = len(ours)
    layers, own, width = ours[0].shape
    size = block_of(width, 12288)
    per = width // size
    specs = [
        pl.BlockSpec(
            (layers, own, size), lambda i, k=k: (0, 0, jnp.clip(i - k * per, 0, per - 1))
        )
        for k in range(streams)
    ]
    summed = jax.ShapeDtypeStruct(ours[0].shape, jnp.float32)
    *grads, squares = pl.pallas_call(
        functools.partial(last_kernel, streams),
        grid=(streams * per,),
        in_specs=[spec for spec in specs for _ in range(3)],
        out_specs=specs + [pl.BlockSpec((own, lanes), lambda i: (0, 0))],
        out_shape=[summed] * streams + [jax.ShapeDtypeStruct((own, lanes), jnp.float32)],
        compiler_params=room,
        cost_estimate=cost_of(*[summed] * (4 * streams)),
        name="last_sums",
    )(*[array for k in range(streams) for array in (ours[k], *sent[k])])
    return grads, squares


def shard_sum(body, shards, which, keep, theirs, *arrived, after=()):
    _, layers, own, width = keep.shape
    size = block_of(width, 6144)
    chosen = pl.BlockSpec((1, layers, own, size), lambda i, shards: (shards[which], 0, 0, i))
    layer = pl.BlockSpec((1, own, size), lambda i, shards: (shards[which], 0, i))
    whole = pl.BlockSpec((layers, own, size), lambda i, shards: (0, 0, i))
    summed = jax.ShapeDtypeStruct((layers, own, width), jnp.float32)
    return pl.pallas_call(
        functools.partial(body, layers),
        grid_spec=pltpu.PrefetchScalarGridSpec(
            num_scalar_prefetch=1,
            grid=(width // size,),
            in_specs=[chosen]
            + [layer] * layers
            + [whole] * len(arrived)
            + [pl.BlockSpec(memory_space=pl.ANY)] * len(after),
            out_specs=whole,
        ),
        out_shape=summed,
        compiler_params=room,
        cost_estimate=cost_of(*[summed] * (3 + len(arrived))),
        name="shard_sum",
    )(shards, keep, *theirs, *arrived, *after)


def update_kernel(count, bound, layers, scales_ref, squares_ref, *rest):
    own, old, rest = rest[:3], rest[3 : 3 + 3 * layers], rest[3 + 3 * layers :]
    grads, outs = rest[: 2 * count], rest[2 * count :]
    step = pl.program_id(0)
    per = pl.num_programs(0) // count
    factor = jnp.minimum(
        jnp.float32(1.0), bound / (jnp.sqrt(jnp.sum(squares_ref[...])) + jnp.float32(1e-06))
    )
    for index in range(count):

        @pl.when(step // per == index)
        def _(index=index):
            states = (
                [ref[...] for ref in own],
                [
                    jnp.concatenate([ref[...] for ref in old[k * layers : (k + 1) * layers]])
                    for k in range(3)
                ],
            )
            for who, state in enumerate(states):
                grad = grads[who * count + index][...]
                new = adamw_update(*state, grad, factor, scales_ref[0], scales_ref[1])
                for out_ref, value in zip(outs[3 * who : 3 * who + 3], new):
                    out_ref[...] = value


def update(scales, squares, state, grads, old_copy, old_last, peer_grads, bound):
    layers, own, columns = state[0].shape
    width = grads[0].shape[-1]
    count = len(grads)
    size = block_of(width, 12288)
    per, blocks = width // size, columns // size
    joint = 3 * layers - 1

    def part(first, many):
        return pl.BlockSpec((layers, own, size), lambda i: (0, 0, jnp.clip(i - first, 0, many - 1)))

    def layer(row):
        return pl.BlockSpec((1, own, size), lambda i: (row, 0, i))

    return pl.pallas_call(
        functools.partial(update_kernel, count, bound, layers),
        grid=(blocks,),
        in_specs=[
            pl.BlockSpec(memory_space=pltpu.SMEM),
            pl.BlockSpec(squares.shape, lambda i: (0, 0)),
        ]
        + [part(0, blocks)] * 3
        + [layer(row) for row in range(joint)]
        + [layer(0)]
        + [part(k * per, per) for k in range(count)] * 2,
        out_specs=[part(0, blocks)] * 6,
        out_shape=[jax.ShapeDtypeStruct((layers, own, columns), jnp.float32)] * 6,
        compiler_params=room,
        cost_estimate=cost_of(*[state[0]] * 14),
        name="update",
    )(scales, squares, *state, *[old_copy] * joint, old_last, *grads, *peer_grads)


def joined_kernel(*refs):
    *parts, out_ref = refs
    for index, part_ref in enumerate(parts):
        out_ref[index] = part_ref[0]


def joined(arrays):
    layers, own, columns = arrays[0].shape
    size = block_of(columns, 12288)
    places = [(array, layer) for array in arrays for layer in range(layers)][:-1]
    return pl.pallas_call(
        joined_kernel,
        grid=(columns // size,),
        in_specs=[pl.BlockSpec((1, own, size), lambda i, l=l: (l, 0, i)) for _, l in places],
        out_specs=pl.BlockSpec((len(places), own, size), lambda i: (0, 0, i)),
        out_shape=jax.ShapeDtypeStruct((len(places), own, columns), jnp.float32),
        compiler_params=room,
        cost_estimate=cost_of(*arrays, *arrays),
        name="joined",
    )(*[array for array, _ in places])


def total_of(value, before, later, last):
    peers, groups = lax.axis_size("dp"), lax.axis_size("mp")
    if peers & (peers - 1) or groups & (groups - 1) or peers < 4:
        return lax.psum(value, ("dp", "mp")), before, later, last

    def exchanged(value, axis, members, *bits):
        others = [lax.ppermute(value, axis, [(i, i ^ bit) for i in members]) for bit in bits]
        return sum(others, value)

    value = exchanged(value, "dp", range(peers), 1)
    value, before, later = lax.optimization_barrier((value, before, later))
    value = exchanged(value, "dp", range(peers), 2)
    value, last = lax.optimization_barrier((value, last))
    first = [i for i in range(peers) if not i & 2]
    bit = 4
    while bit < peers:
        if 2 * bit < peers:
            value = exchanged(value, "dp", first, bit, 2 * bit, 3 * bit)
        else:
            value = exchanged(value, "dp", first, bit)
        bit *= 4
    bit = 1
    while bit < groups:
        value = exchanged(value, "mp", range(groups), bit)
        bit *= 2
    passed = lax.ppermute(value, "dp", [(i, i | 2) for i in first])
    return jnp.where(lax.axis_index("dp") & 2 == 0, value, passed), before, later, last


def local(acc_grads, activations, cotangent, params, first_moment, second_moment, step):
    _, layers, rows, columns = acc_grads.shape
    tokens = activations.shape[0]
    peers = lax.axis_size("dp")
    chips = peers // 2
    half = chips // 2
    order = [2 * z for z in range(half)] + [2 * z + 1 for z in reversed(range(half))]

    def hop(by):
        return [
            (2 * order[r] + core, 2 * order[(r + by) % chips] + core)
            for r in range(chips)
            for core in range(2)
        ]

    swap = [(i, i ^ 1) for i in range(peers)]
    onward = [(i, (i + 1) % peers) for i in range(peers)]

    index = lax.axis_index("dp")
    core, chip = index % 2, index // 2
    place = jnp.where(chip % 2 == 0, chip // 2, chips - 1 - chip // 2)
    hops = jnp.arange(half + 1, dtype=jnp.int32)
    tables = [
        jnp.concatenate([jnp.mod(place + by * hops, chips), core.reshape(1)]) for by in (1, -1)
    ]

    state = (params, first_moment, second_moment)
    old_copy = lax.ppermute(joined(state), "dp", onward)

    same = jnp.eye(layers, dtype=activations.dtype)
    inputs = activations.transpose(1, 2, 0)[:, :, :, None] * same[:, None, None, :]
    inputs = inputs.reshape(layers * rows, tokens * layers)

    width = columns // streams
    keep, theirs, sent = ([None] * streams for _ in range(3))
    for k in range(streams):
        keep[k], *gives = make_terms(
            core.reshape(1), inputs, acc_grads, cotangent, order, k * width, width
        )
        theirs[k] = [lax.ppermute(give, "dp", swap) for give in gives]
    for k in range(streams):
        total = shard_sum(
            plain_kernel, tables[0], half, keep[k], theirs[k]
        )
        sent[k] = [None, None]
        sent[k][k % 2] = lax.ppermute(total, "dp", hop(-1 if k % 2 else 1))
    waiting = [old_copy]
    final = [None] * (2 * streams)
    for away in range(half - 1, 0, -1):
        for k in range(streams):
            for way, by in enumerate((1, -1)):
                arrived = [] if sent[k][way] is None else [sent[k][way]]
                body = step_kernel if arrived else plain_kernel
                after = []
                if k and not arrived:
                    after, waiting = waiting, after
                total = shard_sum(
                    body, tables[way], away, keep[k], theirs[k], *arrived, after=after
                )
                sent[k][way] = lax.ppermute(total, "dp", hop(by))
                final[k * 2 + way] = total
    ours = [shard_sum(plain_kernel, tables[0], 0, keep[k], theirs[k]) for k in range(streams)]
    left = lax.optimization_barrier((state[-1][-1:], *final))[0]
    old_last = lax.ppermute(left, "dp", onward)
    grads, squares = last_sums(ours, sent)
    squares, old_last, *waiting = total_of(squares, old_last, grads[1:], grads[:1])
    peer_grads = [lax.ppermute(value, "dp", onward) for value in waiting[1] + waiting[0]]
    bound = float((layers * rows * columns * lax.axis_size("mp")) ** 0.5)
    count = step.astype(jnp.float32)
    scales = jnp.concatenate(
        [
            1.0 - jnp.power(jnp.float32(beta_one), count),
            1.0 - jnp.power(jnp.float32(beta_two), count),
        ]
    )
    return tuple(update(scales, squares, state, grads, old_copy, old_last, peer_grads, bound))


def solution(mesh):
    owned = P(None, "dp", "mp")
    return jax.shard_map(
        local,
        mesh=mesh,
        in_specs=(
            P("dp", None, None, "mp"),
            P("dp", None, None),
            P("dp", None, "mp"),
            owned,
            owned,
            owned,
            P(),
        ),
        out_specs=(owned,) * 6,
        check_vma=False,
    )
```

```python
import functools
import math

import jax
import jax.numpy as jnp
from jax import lax
from jax.experimental import pallas as pl
from jax.experimental.pallas import tpu as pltpu
from jax.sharding import PartitionSpec as P

beta_one = 0.9
beta_two = 0.95
learn_rate = 0.1
decay_rate = 0.1
epsilon = 1e-08

streams = 2
lanes = 128
room = pltpu.CompilerParams(vmem_limit_bytes=64*2**20)


def block_of(columns, most):
    best = lanes
    for size in range(lanes, min(columns, most) + 1, lanes):
        if columns % size == 0:
            best = size
    return best


def cost_of(*arrays):
    moved = sum(math.prod(a.shape) * jnp.dtype(a.dtype).itemsize for a in arrays)
    return pl.CostEstimate(flops=0, bytes_accessed=moved, transcendentals=0)


def adamw_update(weights, first, second, grad, factor, first_scale, second_scale):
    scaled = factor * grad
    first_new = beta_one * first + (1.0 - beta_one) * scaled
    second_new = beta_two * second + (1.0 - beta_two) * scaled * scaled
    first_hat = first_new / first_scale
    second_hat = second_new / second_scale
    weights_new = weights - learn_rate * (
        first_hat / (jnp.sqrt(second_hat) + epsilon) + decay_rate * weights
    )
    return (weights_new, first_new, second_new)


def terms_kernel(order, layers, core_ref, inputs_ref, earlier_ref, outgrad_ref, *rest):
    keep_ref, gives = rest[-1 - layers], rest[-layers:]
    core = core_ref[0]
    tokens, _, columns = outgrad_ref.shape
    rows = earlier_ref.shape[2]
    outgrad = outgrad_ref[...].reshape(tokens * layers, columns)
    product = jnp.dot(inputs_ref[...], outgrad, preferred_element_type=jnp.float32)
    chips = len(order)
    for layer in range(layers):
        total = earlier_ref[0, layer].astype(jnp.float32) + product[layer * rows : (layer + 1) * rows]
        term = total.astype(jnp.bfloat16).astype(jnp.float32)
        term = term.reshape(chips, 2, rows // (2 * chips), columns)
        for place, chip in enumerate(order):
            keep_ref[place, layer] = jnp.where(core == 0, term[chip, 0], term[chip, 1])
            gives[layer][place] = jnp.where(core == 0, term[chip, 1], term[chip, 0])


def make_terms(core, inputs, earlier, outgrad, order, start, width):
    _, layers, rows, _ = earlier.shape
    tokens = outgrad.shape[0]
    chips = len(order)
    own = rows // (2 * chips)
    size = block_of(width, 6144)
    first = start // size
    return pl.pallas_call(
        functools.partial(terms_kernel, order, layers),
        grid_spec=pltpu.PrefetchScalarGridSpec(
            num_scalar_prefetch=1,
            grid=(width // size,),
            in_specs=[
                pl.BlockSpec(inputs.shape, lambda i, core: (0, 0)),
                pl.BlockSpec((1, layers, rows, size), lambda i, core: (0, 0, 0, first + i)),
                pl.BlockSpec((tokens, layers, size), lambda i, core: (0, 0, first + i)),
            ],
            out_specs=[pl.BlockSpec((chips, layers, own, size), lambda i, core: (0, 0, 0, i))]
            + [pl.BlockSpec((chips, own, size), lambda i, core: (0, 0, i))] * layers,
        ),
        out_shape=[jax.ShapeDtypeStruct((chips, layers, own, width), jnp.float32)]
        + [jax.ShapeDtypeStruct((chips, own, width), jnp.float32)] * layers,
        compiler_params=room,
        cost_estimate=cost_of(
            jax.ShapeDtypeStruct((layers, rows + tokens, width), earlier.dtype),
            jax.ShapeDtypeStruct((layers, rows, width), jnp.float32),
        ),
        name="terms",
    )(core, inputs, earlier, outgrad)


def both_cores(keep_ref, theirs):
    return jnp.stack([keep_ref[0, layer] + theirs_ref[0] for layer, theirs_ref in enumerate(theirs)])


def plain_kernel(layers, shard_ref, keep_ref, *rest):
    theirs, out_ref = rest[:layers], rest[-1]
    out_ref[...] = both_cores(keep_ref, theirs)


def step_kernel(layers, shard_ref, keep_ref, *rest):
    theirs, arrived_ref, out_ref = rest[:layers], rest[layers], rest[-1]
    out_ref[...] = arrived_ref[...] + both_cores(keep_ref, theirs)


def last_kernel(streams, *refs):
    *refs, squares_ref = refs
    refs, outs = refs[:-streams], refs[-streams:]
    step = pl.program_id(0)
    per = pl.num_programs(0) // streams

    @pl.when(step == 0)
    def _():
        squares_ref[...] = jnp.zeros_like(squares_ref)

    for k in range(streams):

        @pl.when(step // per == k)
        def _(k=k):
            own_ref, up_ref, down_ref = refs[3 * k : 3 * k + 3]
            grad = (up_ref[...] + down_ref[...]) + own_ref[...]
            outs[k][...] = grad
            layers, own, columns = grad.shape
            squares = (grad * grad).reshape(layers, own, columns // lanes, lanes)
            squares_ref[...] += jnp.sum(squares, axis=(0, 2))


def last_sums(ours, sent):
    streams = len(ours)
    layers, own, width = ours[0].shape
    size = block_of(width, 12288)
    per = width // size
    specs = [
        pl.BlockSpec(
            (layers, own, size), lambda i, k=k: (0, 0, jnp.clip(i - k * per, 0, per - 1))
        )
        for k in range(streams)
    ]
    summed = jax.ShapeDtypeStruct(ours[0].shape, jnp.float32)
    *grads, squares = pl.pallas_call(
        functools.partial(last_kernel, streams),
        grid=(streams * per,),
        in_specs=[spec for spec in specs for _ in range(3)],
        out_specs=specs + [pl.BlockSpec((own, lanes), lambda i: (0, 0))],
        out_shape=[summed] * streams + [jax.ShapeDtypeStruct((own, lanes), jnp.float32)],
        compiler_params=room,
        cost_estimate=cost_of(*[summed] * (4 * streams)),
        name="last_sums",
    )(*[array for k in range(streams) for array in (ours[k], *sent[k])])
    return grads, squares


def shard_sum(body, shards, which, keep, theirs, *arrived, after=()):
    _, layers, own, width = keep.shape
    size = block_of(width, 6144)
    chosen = pl.BlockSpec((1, layers, own, size), lambda i, shards: (shards[which], 0, 0, i))
    layer = pl.BlockSpec((1, own, size), lambda i, shards: (shards[which], 0, i))
    whole = pl.BlockSpec((layers, own, size), lambda i, shards: (0, 0, i))
    summed = jax.ShapeDtypeStruct((layers, own, width), jnp.float32)
    return pl.pallas_call(
        functools.partial(body, layers),
        grid_spec=pltpu.PrefetchScalarGridSpec(
            num_scalar_prefetch=1,
            grid=(width // size,),
            in_specs=[chosen]
            + [layer] * layers
            + [whole] * len(arrived)
            + [pl.BlockSpec(memory_space=pl.ANY)] * len(after),
            out_specs=whole,
        ),
        out_shape=summed,
        compiler_params=room,
        cost_estimate=cost_of(*[summed] * (3 + len(arrived))),
        name="shard_sum",
    )(shards, keep, *theirs, *arrived, *after)


def update_kernel(count, bound, layers, scales_ref, squares_ref, *rest):
    own, old, rest = rest[:3], rest[3 : 3 + 3 * layers], rest[3 + 3 * layers :]
    grads, outs = rest[: 2 * count], rest[2 * count :]
    step = pl.program_id(0)
    per = pl.num_programs(0) // count
    factor = jnp.minimum(
        jnp.float32(1.0), bound / (jnp.sqrt(jnp.sum(squares_ref[...])) + jnp.float32(1e-06))
    )
    for index in range(count):

        @pl.when(step // per == index)
        def _(index=index):
            states = (
                [ref[...] for ref in own],
                [
                    jnp.concatenate([ref[...] for ref in old[k * layers : (k + 1) * layers]])
                    for k in range(3)
                ],
            )
            for who, state in enumerate(states):
                grad = grads[who * count + index][...]
                new = adamw_update(*state, grad, factor, scales_ref[0], scales_ref[1])
                for out_ref, value in zip(outs[3 * who : 3 * who + 3], new):
                    out_ref[...] = value


def update(scales, squares, state, grads, old_copy, old_last, peer_grads, bound):
    layers, own, columns = state[0].shape
    width = grads[0].shape[-1]
    count = len(grads)
    size = block_of(width, 12288)
    per, blocks = width // size, columns // size
    joint = 3 * layers - 1

    def part(first, many):
        return pl.BlockSpec((layers, own, size), lambda i: (0, 0, jnp.clip(i - first, 0, many - 1)))

    def layer(row):
        return pl.BlockSpec((1, own, size), lambda i: (row, 0, i))

    return pl.pallas_call(
        functools.partial(update_kernel, count, bound, layers),
        grid=(blocks,),
        in_specs=[
            pl.BlockSpec(memory_space=pltpu.SMEM),
            pl.BlockSpec(squares.shape, lambda i: (0, 0)),
        ]
        + [part(0, blocks)] * 3
        + [layer(row) for row in range(joint)]
        + [layer(0)]
        + [part(k * per, per) for k in range(count)] * 2,
        out_specs=[part(0, blocks)] * 6,
        out_shape=[jax.ShapeDtypeStruct((layers, own, columns), jnp.float32)] * 6,
        compiler_params=room,
        cost_estimate=cost_of(*[state[0]] * 14),
        name="update",
    )(scales, squares, *state, *[old_copy] * joint, old_last, *grads, *peer_grads)


def joined_kernel(*refs):
    *parts, out_ref, left_ref = refs
    for index, part_ref in enumerate(parts[:-1]):
        out_ref[index] = part_ref[0]
    left_ref[...] = parts[-1][...]


def joined(arrays):
    layers, own, columns = arrays[0].shape
    size = block_of(columns, 12288)
    places = [(array, layer) for array in arrays for layer in range(layers)]
    joint = len(places) - 1
    return pl.pallas_call(
        joined_kernel,
        grid=(columns // size,),
        in_specs=[pl.BlockSpec((1, own, size), lambda i, l=l: (l, 0, i)) for _, l in places],
        out_specs=[pl.BlockSpec((n, own, size), lambda i: (0, 0, i)) for n in (joint, 1)],
        out_shape=[jax.ShapeDtypeStruct((n, own, columns), jnp.float32) for n in (joint, 1)],
        compiler_params=room,
        cost_estimate=cost_of(*arrays, *arrays),
        name="joined",
    )(*[array for array, _ in places])


def total_of(value, before, later, last):
    peers, groups = lax.axis_size("dp"), lax.axis_size("mp")
    if peers & (peers - 1) or groups & (groups - 1) or peers < 4:
        return lax.psum(value, ("dp", "mp")), before, later, last

    def exchanged(value, axis, members, *bits):
        others = [lax.ppermute(value, axis, [(i, i ^ bit) for i in members]) for bit in bits]
        return sum(others, value)

    value = exchanged(value, "dp", range(peers), 1)
    value, before, later = lax.optimization_barrier((value, before, later))
    value = exchanged(value, "dp", range(peers), 2)
    value, last = lax.optimization_barrier((value, last))
    first = [i for i in range(peers) if not i & 2]
    bit = 4
    while bit < peers:
        if 2 * bit < peers:
            value = exchanged(value, "dp", first, bit, 2 * bit, 3 * bit)
        else:
            value = exchanged(value, "dp", first, bit)
        bit *= 4
    bit = 1
    while bit < groups:
        value = exchanged(value, "mp", range(groups), bit)
        bit *= 2
    passed = lax.ppermute(value, "dp", [(i, i | 2) for i in first])
    return jnp.where(lax.axis_index("dp") & 2 == 0, value, passed), before, later, last


def local(acc_grads, activations, cotangent, params, first_moment, second_moment, step):
    _, layers, rows, columns = acc_grads.shape
    tokens = activations.shape[0]
    peers = lax.axis_size("dp")
    chips = peers // 2
    half = chips // 2
    order = [2 * z for z in range(half)] + [2 * z + 1 for z in reversed(range(half))]

    def hop(by):
        return [
            (2 * order[r] + core, 2 * order[(r + by) % chips] + core)
            for r in range(chips)
            for core in range(2)
        ]

    swap = [(i, i ^ 1) for i in range(peers)]
    onward = [(i, (i + 1) % peers) for i in range(peers)]

    index = lax.axis_index("dp")
    core, chip = index % 2, index // 2
    place = jnp.where(chip % 2 == 0, chip // 2, chips - 1 - chip // 2)
    hops = jnp.arange(half + 1, dtype=jnp.int32)
    tables = [
        jnp.concatenate([jnp.mod(place + by * hops, chips), core.reshape(1)]) for by in (1, -1)
    ]

    state = (params, first_moment, second_moment)
    most, left = joined(state)
    old_copy = lax.ppermute(most, "dp", onward)

    same = jnp.eye(layers, dtype=activations.dtype)
    inputs = activations.transpose(1, 2, 0)[:, :, :, None] * same[:, None, None, :]
    inputs = inputs.reshape(layers * rows, tokens * layers)

    width = columns // streams
    keep, theirs, sent = ([None] * streams for _ in range(3))
    for k in range(streams):
        keep[k], *gives = make_terms(
            core.reshape(1), inputs, acc_grads, cotangent, order, k * width, width
        )
        theirs[k] = [lax.ppermute(give, "dp", swap) for give in gives]
    for k in range(streams):
        total = shard_sum(
            plain_kernel, tables[0], half, keep[k], theirs[k]
        )
        sent[k] = [None, None]
        sent[k][k % 2] = lax.ppermute(total, "dp", hop(-1 if k % 2 else 1))
    waiting = [old_copy]
    for away in range(half - 1, 0, -1):
        for k in range(streams):
            for way, by in enumerate((1, -1)):
                arrived = [] if sent[k][way] is None else [sent[k][way]]
                body = step_kernel if arrived else plain_kernel
                after = []
                if k and not arrived:
                    after, waiting = waiting, after
                total = shard_sum(
                    body, tables[way], away, keep[k], theirs[k], *arrived, after=after
                )
                sent[k][way] = lax.ppermute(total, "dp", hop(by))
    ours = [shard_sum(plain_kernel, tables[0], 0, keep[k], theirs[k]) for k in range(streams)]
    left, *_ = lax.optimization_barrier((left, sent, ours))
    old_last = lax.ppermute(left, "dp", onward)
    grads, squares = last_sums(ours, sent)
    squares, old_last, *waiting = total_of(squares, old_last, grads[1:], grads[:1])
    peer_grads = [lax.ppermute(value, "dp", onward) for value in waiting[1] + waiting[0]]
    bound = float((layers * rows * columns * lax.axis_size("mp")) ** 0.5)
    count = step.astype(jnp.float32)
    scales = jnp.concatenate(
        [
            1.0 - jnp.power(jnp.float32(beta_one), count),
            1.0 - jnp.power(jnp.float32(beta_two), count),
        ]
    )
    return tuple(update(scales, squares, state, grads, old_copy, old_last, peer_grads, bound))


def solution(mesh):
    owned = P(None, "dp", "mp")
    return jax.shard_map(
        local,
        mesh=mesh,
        in_specs=(
            P("dp", None, None, "mp"),
            P("dp", None, None),
            P("dp", None, "mp"),
            owned,
            owned,
            owned,
            P(),
        ),
        out_specs=(owned,) * 6,
        check_vma=False,
    )
```

```python
import functools
import math

import jax
import jax.numpy as jnp
from jax import lax
from jax.experimental import pallas as pl
from jax.experimental.pallas import tpu as pltpu
from jax.sharding import PartitionSpec as P

beta_one = 0.9
beta_two = 0.95
learn_rate = 0.1
decay_rate = 0.1
epsilon = 1e-08

streams = 2
lanes = 128
room = pltpu.CompilerParams(vmem_limit_bytes=64*2**20)


def block_of(columns, most):
    best = lanes
    for size in range(lanes, min(columns, most) + 1, lanes):
        if columns % size == 0:
            best = size
    return best


def cost_of(*arrays):
    moved = sum(math.prod(a.shape) * jnp.dtype(a.dtype).itemsize for a in arrays)
    return pl.CostEstimate(flops=0, bytes_accessed=moved, transcendentals=0)


def adamw_update(weights, first, second, grad, factor, first_scale, second_scale):
    scaled = factor * grad
    first_new = beta_one * first + (1.0 - beta_one) * scaled
    second_new = beta_two * second + (1.0 - beta_two) * scaled * scaled
    first_hat = first_new / first_scale
    second_hat = second_new / second_scale
    weights_new = weights - learn_rate * (
        first_hat / (jnp.sqrt(second_hat) + epsilon) + decay_rate * weights
    )
    return (weights_new, first_new, second_new)


def terms_kernel(order, layers, core_ref, inputs_ref, earlier_ref, outgrad_ref, *rest):
    keep_ref, gives = rest[-1 - layers], rest[-layers:]
    core = core_ref[0]
    tokens, _, columns = outgrad_ref.shape
    rows = earlier_ref.shape[2]
    outgrad = outgrad_ref[...].reshape(tokens * layers, columns)
    product = jnp.dot(inputs_ref[...], outgrad, preferred_element_type=jnp.float32)
    chips = len(order)
    for layer in range(layers):
        total = earlier_ref[0, layer].astype(jnp.float32) + product[layer * rows : (layer + 1) * rows]
        term = total.astype(jnp.bfloat16).astype(jnp.float32)
        term = term.reshape(chips, 2, rows // (2 * chips), columns)
        for place, chip in enumerate(order):
            keep_ref[place, layer] = jnp.where(core == 0, term[chip, 0], term[chip, 1])
            gives[layer][place] = jnp.where(core == 0, term[chip, 1], term[chip, 0])


def make_terms(core, inputs, earlier, outgrad, order, start, width):
    _, layers, rows, _ = earlier.shape
    tokens = outgrad.shape[0]
    chips = len(order)
    own = rows // (2 * chips)
    size = block_of(width, 6144)
    first = start // size
    return pl.pallas_call(
        functools.partial(terms_kernel, order, layers),
        grid_spec=pltpu.PrefetchScalarGridSpec(
            num_scalar_prefetch=1,
            grid=(width // size,),
            in_specs=[
                pl.BlockSpec(inputs.shape, lambda i, core: (0, 0)),
                pl.BlockSpec((1, layers, rows, size), lambda i, core: (0, 0, 0, first + i)),
                pl.BlockSpec((tokens, layers, size), lambda i, core: (0, 0, first + i)),
            ],
            out_specs=[pl.BlockSpec((chips, layers, own, size), lambda i, core: (0, 0, 0, i))]
            + [pl.BlockSpec((chips, own, size), lambda i, core: (0, 0, i))] * layers,
        ),
        out_shape=[jax.ShapeDtypeStruct((chips, layers, own, width), jnp.float32)]
        + [jax.ShapeDtypeStruct((chips, own, width), jnp.float32)] * layers,
        compiler_params=room,
        cost_estimate=cost_of(
            jax.ShapeDtypeStruct((layers, rows + tokens, width), earlier.dtype),
            jax.ShapeDtypeStruct((layers, rows, width), jnp.float32),
        ),
        name="terms",
    )(core, inputs, earlier, outgrad)


def both_cores(keep_ref, theirs):
    return jnp.stack([keep_ref[0, layer] + theirs_ref[0] for layer, theirs_ref in enumerate(theirs)])


def plain_kernel(layers, shard_ref, keep_ref, *rest):
    theirs, out_ref = rest[:layers], rest[-1]
    out_ref[...] = both_cores(keep_ref, theirs)


def step_kernel(layers, shard_ref, keep_ref, *rest):
    theirs, arrived_ref, out_ref = rest[:layers], rest[layers], rest[-1]
    out_ref[...] = arrived_ref[...] + both_cores(keep_ref, theirs)


def last_kernel(streams, *refs):
    *refs, squares_ref = refs
    refs, outs = refs[:-streams], refs[-streams:]
    step = pl.program_id(0)
    per = pl.num_programs(0) // streams

    @pl.when(step == 0)
    def _():
        squares_ref[...] = jnp.zeros_like(squares_ref)

    for k in range(streams):

        @pl.when(step // per == k)
        def _(k=k):
            own_ref, up_ref, down_ref = refs[3 * k : 3 * k + 3]
            grad = (up_ref[...] + down_ref[...]) + own_ref[...]
            outs[k][...] = grad
            layers, own, columns = grad.shape
            squares = (grad * grad).reshape(layers, own, columns // lanes, lanes)
            squares_ref[...] += jnp.sum(squares, axis=(0, 2))


def last_sums(ours, sent):
    streams = len(ours)
    layers, own, width = ours[0].shape
    size = block_of(width, 12288)
    per = width // size
    specs = [
        pl.BlockSpec(
            (layers, own, size), lambda i, k=k: (0, 0, jnp.clip(i - k * per, 0, per - 1))
        )
        for k in range(streams)
    ]
    summed = jax.ShapeDtypeStruct(ours[0].shape, jnp.float32)
    *grads, squares = pl.pallas_call(
        functools.partial(last_kernel, streams),
        grid=(streams * per,),
        in_specs=[spec for spec in specs for _ in range(3)],
        out_specs=specs + [pl.BlockSpec((own, lanes), lambda i: (0, 0))],
        out_shape=[summed] * streams + [jax.ShapeDtypeStruct((own, lanes), jnp.float32)],
        compiler_params=room,
        cost_estimate=cost_of(*[summed] * (4 * streams)),
        name="last_sums",
    )(*[array for k in range(streams) for array in (ours[k], *sent[k])])
    return grads, squares


def shard_sum(body, shards, which, keep, theirs, *arrived, after=()):
    _, layers, own, width = keep.shape
    size = block_of(width, 6144)
    chosen = pl.BlockSpec((1, layers, own, size), lambda i, shards: (shards[which], 0, 0, i))
    layer = pl.BlockSpec((1, own, size), lambda i, shards: (shards[which], 0, i))
    whole = pl.BlockSpec((layers, own, size), lambda i, shards: (0, 0, i))
    summed = jax.ShapeDtypeStruct((layers, own, width), jnp.float32)
    return pl.pallas_call(
        functools.partial(body, layers),
        grid_spec=pltpu.PrefetchScalarGridSpec(
            num_scalar_prefetch=1,
            grid=(width // size,),
            in_specs=[chosen]
            + [layer] * layers
            + [whole] * len(arrived)
            + [pl.BlockSpec(memory_space=pl.ANY)] * len(after),
            out_specs=whole,
        ),
        out_shape=summed,
        compiler_params=room,
        cost_estimate=cost_of(*[summed] * (3 + len(arrived))),
        name="shard_sum",
    )(shards, keep, *theirs, *arrived, *after)


def update_kernel(count, bound, layers, scales_ref, squares_ref, *rest):
    own, old, rest = rest[:3], rest[3 : 3 + 3 * layers], rest[3 + 3 * layers :]
    grads, outs = rest[: 2 * count], rest[2 * count :]
    step = pl.program_id(0)
    per = pl.num_programs(0) // count
    factor = jnp.minimum(
        jnp.float32(1.0), bound / (jnp.sqrt(jnp.sum(squares_ref[...])) + jnp.float32(1e-06))
    )
    for index in range(count):

        @pl.when(step // per == index)
        def _(index=index):
            states = (
                [ref[...] for ref in own],
                [
                    jnp.concatenate([ref[...] for ref in old[k * layers : (k + 1) * layers]])
                    for k in range(3)
                ],
            )
            for who, state in enumerate(states):
                grad = grads[who * count + index][...]
                new = adamw_update(*state, grad, factor, scales_ref[0], scales_ref[1])
                for out_ref, value in zip(outs[3 * who : 3 * who + 3], new):
                    out_ref[...] = value


def update(scales, squares, state, grads, old_copy, old_last, peer_grads, bound):
    layers, own, columns = state[0].shape
    width = grads[0].shape[-1]
    count = len(grads)
    size = block_of(width, 12288)
    per, blocks = width // size, columns // size
    joint = 3 * layers - 1

    def part(first, many):
        return pl.BlockSpec((layers, own, size), lambda i: (0, 0, jnp.clip(i - first, 0, many - 1)))

    def layer(row):
        return pl.BlockSpec((1, own, size), lambda i: (row, 0, i))

    return pl.pallas_call(
        functools.partial(update_kernel, count, bound, layers),
        grid=(blocks,),
        in_specs=[
            pl.BlockSpec(memory_space=pltpu.SMEM),
            pl.BlockSpec(squares.shape, lambda i: (0, 0)),
        ]
        + [part(0, blocks)] * 3
        + [layer(row) for row in range(joint)]
        + [layer(0)]
        + [part(k * per, per) for k in range(count)] * 2,
        out_specs=[part(0, blocks)] * 6,
        out_shape=[jax.ShapeDtypeStruct((layers, own, columns), jnp.float32)] * 6,
        compiler_params=room,
        cost_estimate=cost_of(*[state[0]] * 14),
        name="update",
    )(scales, squares, *state, *[old_copy] * joint, old_last, *grads, *peer_grads)


def joined_kernel(*refs):
    *parts, out_ref, left_ref = refs
    for index, part_ref in enumerate(parts[:-1]):
        out_ref[index] = part_ref[0]
    left_ref[...] = parts[-1][...]


def joined(arrays):
    layers, own, columns = arrays[0].shape
    size = block_of(columns, 12288)
    places = [(array, layer) for array in arrays for layer in range(layers)]
    joint = len(places) - 1
    return pl.pallas_call(
        joined_kernel,
        grid=(columns // size,),
        in_specs=[pl.BlockSpec((1, own, size), lambda i, l=l: (l, 0, i)) for _, l in places],
        out_specs=[pl.BlockSpec((n, own, size), lambda i: (0, 0, i)) for n in (joint, 1)],
        out_shape=[jax.ShapeDtypeStruct((n, own, columns), jnp.float32) for n in (joint, 1)],
        compiler_params=room,
        cost_estimate=cost_of(*arrays, *arrays),
        name="joined",
    )(*[array for array, _ in places])


def total_of(value, before, later, last):
    peers, groups = lax.axis_size("dp"), lax.axis_size("mp")
    if peers & (peers - 1) or groups & (groups - 1) or peers < 4:
        return lax.psum(value, ("dp", "mp")), before, later, last

    def exchanged(value, axis, members, *bits):
        others = [lax.ppermute(value, axis, [(i, i ^ bit) for i in members]) for bit in bits]
        return sum(others, value)

    value = exchanged(value, "dp", range(peers), 1)
    value, before, later = lax.optimization_barrier((value, before, later))
    value = exchanged(value, "dp", range(peers), 2)
    value, last = lax.optimization_barrier((value, last))
    first = [i for i in range(peers) if not i & 2]
    bit = 4
    while bit < peers:
        if 2 * bit < peers:
            value = exchanged(value, "dp", first, bit, 2 * bit, 3 * bit)
        else:
            value = exchanged(value, "dp", first, bit)
        bit *= 4
    bit = 1
    while bit < groups:
        value = exchanged(value, "mp", range(groups), bit)
        bit *= 2
    passed = lax.ppermute(value, "dp", [(i, i | 2) for i in first])
    return jnp.where(lax.axis_index("dp") & 2 == 0, value, passed), before, later, last


def local(acc_grads, activations, cotangent, params, first_moment, second_moment, step):
    _, layers, rows, columns = acc_grads.shape
    tokens = activations.shape[0]
    peers = lax.axis_size("dp")
    chips = peers // 2
    half = chips // 2
    order = [2 * z for z in range(half)] + [2 * z + 1 for z in reversed(range(half))]

    def hop(by):
        return [
            (2 * order[r] + core, 2 * order[(r + by) % chips] + core)
            for r in range(chips)
            for core in range(2)
        ]

    swap = [(i, i ^ 1) for i in range(peers)]
    onward = [(i, (i + 1) % peers) for i in range(peers)]

    index = lax.axis_index("dp")
    core, chip = index % 2, index // 2
    place = jnp.where(chip % 2 == 0, chip // 2, chips - 1 - chip // 2)
    hops = jnp.arange(half + 1, dtype=jnp.int32)
    tables = [
        jnp.concatenate([jnp.mod(place + by * hops, chips), core.reshape(1)]) for by in (1, -1)
    ]

    state = (params, first_moment, second_moment)
    most, left = joined(state)
    old_copy = lax.ppermute(most, "dp", onward)

    same = jnp.eye(layers, dtype=activations.dtype)
    inputs = activations.transpose(1, 2, 0)[:, :, :, None] * same[:, None, None, :]
    inputs = inputs.reshape(layers * rows, tokens * layers)

    width = columns // streams
    keep, theirs, sent = ([None] * streams for _ in range(3))
    for k in range(streams):
        keep[k], *gives = make_terms(
            core.reshape(1), inputs, acc_grads, cotangent, order, k * width, width
        )
        theirs[k] = [lax.ppermute(give, "dp", swap) for give in gives]
    for k in range(streams):
        total = shard_sum(
            plain_kernel, tables[0], half, keep[k], theirs[k], after=[old_copy] if k else []
        )
        sent[k] = [None, None]
        sent[k][k % 2] = lax.ppermute(total, "dp", hop(-1 if k % 2 else 1))
    for away in range(half - 1, 0, -1):
        for k in range(streams):
            for way, by in enumerate((1, -1)):
                arrived = [] if sent[k][way] is None else [sent[k][way]]
                body = step_kernel if arrived else plain_kernel
                total = shard_sum(body, tables[way], away, keep[k], theirs[k], *arrived)
                sent[k][way] = lax.ppermute(total, "dp", hop(by))
    ours = [shard_sum(plain_kernel, tables[0], 0, keep[k], theirs[k]) for k in range(streams)]
    grads, squares = last_sums(ours, sent)
    left, squares = lax.optimization_barrier((left, squares))
    old_last = lax.ppermute(left, "dp", onward)
    squares, old_last, *waiting = total_of(squares, old_last, grads[1:], grads[:1])
    peer_grads = [lax.ppermute(value, "dp", onward) for value in waiting[1] + waiting[0]]
    bound = float((layers * rows * columns * lax.axis_size("mp")) ** 0.5)
    count = step.astype(jnp.float32)
    scales = jnp.concatenate(
        [
            1.0 - jnp.power(jnp.float32(beta_one), count),
            1.0 - jnp.power(jnp.float32(beta_two), count),
        ]
    )
    return tuple(update(scales, squares, state, grads, old_copy, old_last, peer_grads, bound))


def solution(mesh):
    owned = P(None, "dp", "mp")
    return jax.shard_map(
        local,
        mesh=mesh,
        in_specs=(
            P("dp", None, None, "mp"),
            P("dp", None, None),
            P("dp", None, "mp"),
            owned,
            owned,
            owned,
            P(),
        ),
        out_specs=(owned,) * 6,
        check_vma=False,
    )
```

```python
import functools
import math

import jax
import jax.numpy as jnp
from jax import lax
from jax.experimental import pallas as pl
from jax.experimental.pallas import tpu as pltpu
from jax.sharding import PartitionSpec as P

beta_one = 0.9
beta_two = 0.95
learn_rate = 0.1
decay_rate = 0.1
epsilon = 1e-08

streams = 2
lanes = 128
room = pltpu.CompilerParams(vmem_limit_bytes=64*2**20)


def block_of(columns, most):
    best = lanes
    for size in range(lanes, min(columns, most) + 1, lanes):
        if columns % size == 0:
            best = size
    return best


def cost_of(*arrays):
    moved = sum(math.prod(a.shape) * jnp.dtype(a.dtype).itemsize for a in arrays)
    return pl.CostEstimate(flops=0, bytes_accessed=moved, transcendentals=0)


def adamw_update(weights, first, second, grad, factor, first_scale, second_scale):
    scaled = factor * grad
    first_new = beta_one * first + (1.0 - beta_one) * scaled
    second_new = beta_two * second + (1.0 - beta_two) * scaled * scaled
    first_hat = first_new / first_scale
    second_hat = second_new / second_scale
    weights_new = weights - learn_rate * (
        first_hat / (jnp.sqrt(second_hat) + epsilon) + decay_rate * weights
    )
    return (weights_new, first_new, second_new)


def terms_kernel(order, layers, core_ref, inputs_ref, earlier_ref, outgrad_ref, *rest):
    keep_ref, gives = rest[-1 - layers], rest[-layers:]
    core = core_ref[0]
    tokens, _, columns = outgrad_ref.shape
    rows = earlier_ref.shape[2]
    outgrad = outgrad_ref[...].reshape(tokens * layers, columns)
    product = jnp.dot(inputs_ref[...], outgrad, preferred_element_type=jnp.float32)
    chips = len(order)
    for layer in range(layers):
        total = earlier_ref[0, layer].astype(jnp.float32) + product[layer * rows : (layer + 1) * rows]
        term = total.astype(jnp.bfloat16).astype(jnp.float32)
        term = term.reshape(chips, 2, rows // (2 * chips), columns)
        for place, chip in enumerate(order):
            keep_ref[place, layer] = jnp.where(core == 0, term[chip, 0], term[chip, 1])
            gives[layer][place] = jnp.where(core == 0, term[chip, 1], term[chip, 0])


def make_terms(core, inputs, earlier, outgrad, order, start, width):
    _, layers, rows, _ = earlier.shape
    tokens = outgrad.shape[0]
    chips = len(order)
    own = rows // (2 * chips)
    size = block_of(width, 6144)
    first = start // size
    return pl.pallas_call(
        functools.partial(terms_kernel, order, layers),
        grid_spec=pltpu.PrefetchScalarGridSpec(
            num_scalar_prefetch=1,
            grid=(width // size,),
            in_specs=[
                pl.BlockSpec(inputs.shape, lambda i, core: (0, 0)),
                pl.BlockSpec((1, layers, rows, size), lambda i, core: (0, 0, 0, first + i)),
                pl.BlockSpec((tokens, layers, size), lambda i, core: (0, 0, first + i)),
            ],
            out_specs=[pl.BlockSpec((chips, layers, own, size), lambda i, core: (0, 0, 0, i))]
            + [pl.BlockSpec((chips, own, size), lambda i, core: (0, 0, i))] * layers,
        ),
        out_shape=[jax.ShapeDtypeStruct((chips, layers, own, width), jnp.float32)]
        + [jax.ShapeDtypeStruct((chips, own, width), jnp.float32)] * layers,
        compiler_params=room,
        cost_estimate=cost_of(
            jax.ShapeDtypeStruct((layers, rows + tokens, width), earlier.dtype),
            jax.ShapeDtypeStruct((layers, rows, width), jnp.float32),
        ),
        name="terms",
    )(core, inputs, earlier, outgrad)


def both_cores(keep_ref, theirs):
    return jnp.stack([keep_ref[0, layer] + theirs_ref[0] for layer, theirs_ref in enumerate(theirs)])


def plain_kernel(layers, shard_ref, keep_ref, *rest):
    theirs, out_ref = rest[:layers], rest[-1]
    out_ref[...] = both_cores(keep_ref, theirs)


def step_kernel(layers, shard_ref, keep_ref, *rest):
    theirs, arrived_ref, out_ref = rest[:layers], rest[layers], rest[-1]
    out_ref[...] = arrived_ref[...] + both_cores(keep_ref, theirs)


def last_kernel(streams, *refs):
    *refs, squares_ref = refs
    refs, outs = refs[:-streams], refs[-streams:]
    step = pl.program_id(0)
    per = pl.num_programs(0) // streams

    @pl.when(step == 0)
    def _():
        squares_ref[...] = jnp.zeros_like(squares_ref)

    for k in range(streams):

        @pl.when(step // per == k)
        def _(k=k):
            own_ref, up_ref, down_ref = refs[3 * k : 3 * k + 3]
            grad = (up_ref[...] + down_ref[...]) + own_ref[...]
            outs[k][...] = grad
            layers, own, columns = grad.shape
            squares = (grad * grad).reshape(layers, own, columns // lanes, lanes)
            squares_ref[...] += jnp.sum(squares, axis=(0, 2))


def last_sums(ours, sent):
    streams = len(ours)
    layers, own, width = ours[0].shape
    size = block_of(width, 12288)
    per = width // size
    specs = [
        pl.BlockSpec(
            (layers, own, size), lambda i, k=k: (0, 0, jnp.clip(i - k * per, 0, per - 1))
        )
        for k in range(streams)
    ]
    summed = jax.ShapeDtypeStruct(ours[0].shape, jnp.float32)
    *grads, squares = pl.pallas_call(
        functools.partial(last_kernel, streams),
        grid=(streams * per,),
        in_specs=[spec for spec in specs for _ in range(3)],
        out_specs=specs + [pl.BlockSpec((own, lanes), lambda i: (0, 0))],
        out_shape=[summed] * streams + [jax.ShapeDtypeStruct((own, lanes), jnp.float32)],
        compiler_params=room,
        cost_estimate=cost_of(*[summed] * (4 * streams)),
        name="last_sums",
    )(*[array for k in range(streams) for array in (ours[k], *sent[k])])
    return grads, squares


def shard_sum(body, shards, which, keep, theirs, *arrived, after=()):
    _, layers, own, width = keep.shape
    size = block_of(width, 6144)
    chosen = pl.BlockSpec((1, layers, own, size), lambda i, shards: (shards[which], 0, 0, i))
    layer = pl.BlockSpec((1, own, size), lambda i, shards: (shards[which], 0, i))
    whole = pl.BlockSpec((layers, own, size), lambda i, shards: (0, 0, i))
    summed = jax.ShapeDtypeStruct((layers, own, width), jnp.float32)
    return pl.pallas_call(
        functools.partial(body, layers),
        grid_spec=pltpu.PrefetchScalarGridSpec(
            num_scalar_prefetch=1,
            grid=(width // size,),
            in_specs=[chosen]
            + [layer] * layers
            + [whole] * len(arrived)
            + [pl.BlockSpec(memory_space=pl.ANY)] * len(after),
            out_specs=whole,
        ),
        out_shape=summed,
        compiler_params=room,
        cost_estimate=cost_of(*[summed] * (3 + len(arrived))),
        name="shard_sum",
    )(shards, keep, *theirs, *arrived, *after)


def update_kernel(count, bound, scales_ref, squares_ref, *rest):
    states, grads, outs = (rest[:3], rest[3:6]), rest[6 : 6 + 2 * count], rest[6 + 2 * count :]
    step = pl.program_id(0)
    per = pl.num_programs(0) // count
    factor = jnp.minimum(
        jnp.float32(1.0), bound / (jnp.sqrt(jnp.sum(squares_ref[...])) + jnp.float32(1e-06))
    )
    for index in range(count):

        @pl.when(step // per == index)
        def _(index=index):
            for who in range(2):
                new = adamw_update(
                    *[ref[...] for ref in states[who]],
                    grads[who * count + index][...],
                    factor,
                    scales_ref[0],
                    scales_ref[1],
                )
                for out_ref, value in zip(outs[3 * who : 3 * who + 3], new):
                    out_ref[...] = value


def update(scales, squares, state, grads, old_copy, peer_grads, bound):
    layers, own, columns = state[0].shape
    width = grads[0].shape[-1]
    count = len(grads)
    size = block_of(width, 12288)
    per, blocks = width // size, columns // size
    shape = (layers, own, size)

    def part(first, many, row=0):
        return pl.BlockSpec(shape, lambda i: (row, 0, jnp.clip(i - first, 0, many - 1)))

    return pl.pallas_call(
        functools.partial(update_kernel, count, bound),
        grid=(blocks,),
        in_specs=[
            pl.BlockSpec(memory_space=pltpu.SMEM),
            pl.BlockSpec(squares.shape, lambda i: (0, 0)),
        ]
        + [part(0, blocks)] * 3
        + [part(0, blocks, row) for row in range(3)]
        + [part(k * per, per) for k in range(count)] * 2,
        out_specs=[part(0, blocks)] * 6,
        out_shape=[jax.ShapeDtypeStruct((layers, own, columns), jnp.float32)] * 6,
        compiler_params=room,
        cost_estimate=cost_of(*[state[0]] * 14),
        name="update",
    )(scales, squares, *state, *[old_copy] * 3, *grads, *peer_grads)


def joined_kernel(*refs):
    *parts, out_ref = refs
    layers = parts[0].shape[0]
    for index, part_ref in enumerate(parts):
        out_ref[index * layers : (index + 1) * layers] = part_ref[...]


def joined(arrays):
    layers, own, columns = arrays[0].shape
    size = block_of(columns, 12288)
    return pl.pallas_call(
        joined_kernel,
        grid=(columns // size,),
        in_specs=[pl.BlockSpec((layers, own, size), lambda i: (0, 0, i))] * len(arrays),
        out_specs=pl.BlockSpec((len(arrays) * layers, own, size), lambda i: (0, 0, i)),
        out_shape=jax.ShapeDtypeStruct((len(arrays) * layers, own, columns), jnp.float32),
        compiler_params=room,
        cost_estimate=cost_of(*arrays, *arrays),
        name="joined",
    )(*arrays)


def total_of(value, later, last):
    peers, groups = lax.axis_size("dp"), lax.axis_size("mp")
    if peers & (peers - 1) or groups & (groups - 1) or peers < 4:
        return lax.psum(value, ("dp", "mp")), later, last

    def exchanged(value, axis, members, bit):
        return value + lax.ppermute(value, axis, [(i, i ^ bit) for i in members])

    value = exchanged(value, "dp", range(peers), 1)
    value, later = lax.optimization_barrier((value, later))
    value = exchanged(value, "dp", range(peers), 2)
    value, last = lax.optimization_barrier((value, last))
    first = [i for i in range(peers) if not i & 2]
    bit = 4
    while bit < peers:
        value = exchanged(value, "dp", first, bit)
        bit *= 2
    bit = 1
    while bit < groups:
        value = exchanged(value, "mp", range(groups), bit)
        bit *= 2
    passed = lax.ppermute(value, "dp", [(i, i | 2) for i in first])
    return jnp.where(lax.axis_index("dp") & 2 == 0, value, passed), later, last


def local(acc_grads, activations, cotangent, params, first_moment, second_moment, step):
    _, layers, rows, columns = acc_grads.shape
    tokens = activations.shape[0]
    peers = lax.axis_size("dp")
    chips = peers // 2
    half = chips // 2
    order = [2 * z for z in range(half)] + [2 * z + 1 for z in reversed(range(half))]

    def hop(by):
        return [
            (2 * order[r] + core, 2 * order[(r + by) % chips] + core)
            for r in range(chips)
            for core in range(2)
        ]

    swap = [(i, i ^ 1) for i in range(peers)]
    onward = [(i, (i + 1) % peers) for i in range(peers)]

    index = lax.axis_index("dp")
    core, chip = index % 2, index // 2
    place = jnp.where(chip % 2 == 0, chip // 2, chips - 1 - chip // 2)
    hops = jnp.arange(half + 1, dtype=jnp.int32)
    tables = [
        jnp.concatenate([jnp.mod(place + by * hops, chips), core.reshape(1)]) for by in (1, -1)
    ]

    state = (params, first_moment, second_moment)
    old_copy = lax.ppermute(joined(state), "dp", onward)

    same = jnp.eye(layers, dtype=activations.dtype)
    inputs = activations.transpose(1, 2, 0)[:, :, :, None] * same[:, None, None, :]
    inputs = inputs.reshape(layers * rows, tokens * layers)

    width = columns // streams
    keep, theirs, sent = ([None] * streams for _ in range(3))
    for k in range(streams):
        keep[k], *gives = make_terms(
            core.reshape(1), inputs, acc_grads, cotangent, order, k * width, width
        )
        theirs[k] = [lax.ppermute(give, "dp", swap) for give in gives]
    for k in range(streams):
        total = shard_sum(
            plain_kernel, tables[0], half, keep[k], theirs[k]
        )
        sent[k] = [None, None]
        sent[k][k % 2] = lax.ppermute(total, "dp", hop(-1 if k % 2 else 1))
    waiting = [old_copy]
    for away in range(half - 1, 0, -1):
        for k in range(streams):
            for way, by in enumerate((1, -1)):
                arrived = [] if sent[k][way] is None else [sent[k][way]]
                body = step_kernel if arrived else plain_kernel
                after = []
                if arrived:
                    after, waiting = waiting, after
                total = shard_sum(
                    body, tables[way], away, keep[k], theirs[k], *arrived, after=after
                )
                sent[k][way] = lax.ppermute(total, "dp", hop(by))
    ours = [shard_sum(plain_kernel, tables[0], 0, keep[k], theirs[k]) for k in range(streams)]
    grads, squares = last_sums(ours, sent)
    squares, *waiting = total_of(squares, grads[1:], grads[:1])
    peer_grads = [lax.ppermute(value, "dp", onward) for value in waiting[1] + waiting[0]]
    bound = float((layers * rows * columns * lax.axis_size("mp")) ** 0.5)
    count = step.astype(jnp.float32)
    scales = jnp.concatenate(
        [
            1.0 - jnp.power(jnp.float32(beta_one), count),
            1.0 - jnp.power(jnp.float32(beta_two), count),
        ]
    )
    return tuple(update(scales, squares, state, grads, old_copy, peer_grads, bound))


def solution(mesh):
    owned = P(None, "dp", "mp")
    return jax.shard_map(
        local,
        mesh=mesh,
        in_specs=(
            P("dp", None, None, "mp"),
            P("dp", None, None),
            P("dp", None, "mp"),
            owned,
            owned,
            owned,
            P(),
        ),
        out_specs=(owned,) * 6,
        check_vma=False,
    )
```

```python
import functools
import math

import jax
import jax.numpy as jnp
from jax import lax
from jax.experimental import pallas as pl
from jax.experimental.pallas import tpu as pltpu
from jax.sharding import PartitionSpec as P

beta_one = 0.9
beta_two = 0.95
learn_rate = 0.1
decay_rate = 0.1
epsilon = 1e-08

streams = 2
lanes = 128
room = pltpu.CompilerParams(vmem_limit_bytes=64*2**20)


def block_of(columns, most):
    best = lanes
    for size in range(lanes, min(columns, most) + 1, lanes):
        if columns % size == 0:
            best = size
    return best


def cost_of(*arrays):
    moved = sum(math.prod(a.shape) * jnp.dtype(a.dtype).itemsize for a in arrays)
    return pl.CostEstimate(flops=0, bytes_accessed=moved, transcendentals=0)


def adamw_update(weights, first, second, grad, factor, first_scale, second_scale):
    scaled = factor * grad
    first_new = beta_one * first + (1.0 - beta_one) * scaled
    second_new = beta_two * second + (1.0 - beta_two) * scaled * scaled
    first_hat = first_new / first_scale
    second_hat = second_new / second_scale
    weights_new = weights - learn_rate * (
        first_hat / (jnp.sqrt(second_hat) + epsilon) + decay_rate * weights
    )
    return (weights_new, first_new, second_new)


def terms_kernel(order, layers, held, core_ref, inputs_ref, earlier_ref, outgrad_ref, *rest):
    keep_ref, *gives = rest[held:]
    halves = len(gives) // layers
    here = pl.program_id(0) // (pl.num_programs(0) // halves)
    core = core_ref[0]
    tokens, _, columns = outgrad_ref.shape
    rows = earlier_ref.shape[2]
    outgrad = outgrad_ref[...].reshape(tokens * layers, columns)
    product = jnp.dot(inputs_ref[...], outgrad, preferred_element_type=jnp.float32)
    chips = len(order)
    for layer in range(layers):
        total = earlier_ref[0, layer].astype(jnp.float32) + product[layer * rows : (layer + 1) * rows]
        term = total.astype(jnp.bfloat16).astype(jnp.float32)
        term = term.reshape(chips, 2, rows // (2 * chips), columns)
        for place, chip in enumerate(order):
            keep_ref[place, layer] = jnp.where(core == 0, term[chip, 0], term[chip, 1])
            given = jnp.where(core == 0, term[chip, 1], term[chip, 0])
            for index in range(halves):

                @pl.when(here == index)
                def _(index=index, given=given, layer=layer, place=place):
                    gives[layer * halves + index][place] = given


def make_terms(core, inputs, earlier, outgrad, order, start, width, after):
    _, layers, rows, _ = earlier.shape
    tokens = outgrad.shape[0]
    chips = len(order)
    own = rows // (2 * chips)
    half = width // 2
    size = block_of(half, 6144)
    per = half // size
    first = start // size
    return pl.pallas_call(
        functools.partial(terms_kernel, order, layers, len(after)),
        grid_spec=pltpu.PrefetchScalarGridSpec(
            num_scalar_prefetch=1,
            grid=(width // size,),
            in_specs=[
                pl.BlockSpec(inputs.shape, lambda i, core: (0, 0)),
                pl.BlockSpec((1, layers, rows, size), lambda i, core: (0, 0, 0, first + i)),
                pl.BlockSpec((tokens, layers, size), lambda i, core: (0, 0, first + i)),
            ]
            + [pl.BlockSpec(memory_space=pl.ANY)] * len(after),
            out_specs=[pl.BlockSpec((chips, layers, own, size), lambda i, core: (0, 0, 0, i))]
            + [
                pl.BlockSpec(
                    (chips, own, size), lambda i, core, h=h: (0, 0, jnp.clip(i - h * per, 0, per - 1))
                )
                for h in range(2)
            ]
            * layers,
        ),
        out_shape=[jax.ShapeDtypeStruct((chips, layers, own, width), jnp.float32)]
        + [jax.ShapeDtypeStruct((chips, own, half), jnp.float32)] * (2 * layers),
        compiler_params=room,
        cost_estimate=cost_of(
            jax.ShapeDtypeStruct((layers, rows + tokens, width), earlier.dtype),
            jax.ShapeDtypeStruct((layers, rows, width), jnp.float32),
        ),
        name="terms",
    )(core, inputs, earlier, outgrad, *after)


def both_cores(keep_ref, theirs):
    layers = keep_ref.shape[1]
    halves = len(theirs) // layers
    here = pl.program_id(0) // (pl.num_programs(0) // halves)
    rows = []
    for layer in range(layers):
        row = theirs[layer * halves][0]
        for index in range(1, halves):
            row = jnp.where(here == index, theirs[layer * halves + index][0], row)
        rows.append(keep_ref[0, layer] + row)
    return jnp.stack(rows)


def plain_kernel(parts, shard_ref, keep_ref, *rest):
    theirs, out_ref = rest[:parts], rest[-1]
    out_ref[...] = both_cores(keep_ref, theirs)


def step_kernel(parts, shard_ref, keep_ref, *rest):
    theirs, arrived_ref, out_ref = rest[:parts], rest[parts], rest[-1]
    out_ref[...] = arrived_ref[...] + both_cores(keep_ref, theirs)


def last_kernel(streams, *refs):
    *refs, squares_ref = refs
    refs, outs = refs[:-streams], refs[-streams:]
    step = pl.program_id(0)
    per = pl.num_programs(0) // streams

    @pl.when(step == 0)
    def _():
        squares_ref[...] = jnp.zeros_like(squares_ref)

    for k in range(streams):

        @pl.when(step // per == k)
        def _(k=k):
            own_ref, up_ref, down_ref = refs[3 * k : 3 * k + 3]
            grad = (up_ref[...] + down_ref[...]) + own_ref[...]
            outs[k][...] = grad
            layers, own, columns = grad.shape
            squares = (grad * grad).reshape(layers, own, columns // lanes, lanes)
            squares_ref[...] += jnp.sum(squares, axis=(0, 2))


def last_sums(ours, sent):
    streams = len(ours)
    layers, own, width = ours[0].shape
    size = block_of(width, 12288)
    per = width // size
    specs = [
        pl.BlockSpec(
            (layers, own, size), lambda i, k=k: (0, 0, jnp.clip(i - k * per, 0, per - 1))
        )
        for k in range(streams)
    ]
    summed = jax.ShapeDtypeStruct(ours[0].shape, jnp.float32)
    *grads, squares = pl.pallas_call(
        functools.partial(last_kernel, streams),
        grid=(streams * per,),
        in_specs=[spec for spec in specs for _ in range(3)],
        out_specs=specs + [pl.BlockSpec((own, lanes), lambda i: (0, 0))],
        out_shape=[summed] * streams + [jax.ShapeDtypeStruct((own, lanes), jnp.float32)],
        compiler_params=room,
        cost_estimate=cost_of(*[summed] * (4 * streams)),
        name="last_sums",
    )(*[array for k in range(streams) for array in (ours[k], *sent[k])])
    return grads, squares


def shard_sum(body, shards, which, keep, theirs, *arrived, after=()):
    _, layers, own, width = keep.shape
    half = theirs[0].shape[-1]
    size = block_of(half, 6144)
    per, halves = half // size, width // half
    chosen = pl.BlockSpec((1, layers, own, size), lambda i, shards: (shards[which], 0, 0, i))
    pieces = [
        pl.BlockSpec(
            (1, own, size),
            lambda i, shards, h=h: (shards[which], 0, jnp.clip(i - h * per, 0, per - 1)),
        )
        for h in range(halves)
    ]
    whole = pl.BlockSpec((layers, own, size), lambda i, shards: (0, 0, i))
    summed = jax.ShapeDtypeStruct((layers, own, width), jnp.float32)
    return pl.pallas_call(
        functools.partial(body, len(theirs)),
        grid_spec=pltpu.PrefetchScalarGridSpec(
            num_scalar_prefetch=1,
            grid=(width // size,),
            in_specs=[chosen]
            + pieces * layers
            + [whole] * len(arrived)
            + [pl.BlockSpec(memory_space=pl.ANY)] * len(after),
            out_specs=whole,
        ),
        out_shape=summed,
        compiler_params=room,
        cost_estimate=cost_of(*[summed] * (3 + len(arrived))),
        name="shard_sum",
    )(shards, keep, *theirs, *arrived, *after)


def update_kernel(count, bound, scales_ref, squares_ref, *rest):
    states, grads, outs = (rest[:3], rest[3:6]), rest[6 : 6 + 2 * count], rest[6 + 2 * count :]
    step = pl.program_id(0)
    per = pl.num_programs(0) // count
    factor = jnp.minimum(
        jnp.float32(1.0), bound / (jnp.sqrt(jnp.sum(squares_ref[...])) + jnp.float32(1e-06))
    )
    for index in range(count):

        @pl.when(step // per == index)
        def _(index=index):
            for who in range(2):
                new = adamw_update(
                    *[ref[...] for ref in states[who]],
                    grads[who * count + index][...],
                    factor,
                    scales_ref[0],
                    scales_ref[1],
                )
                for out_ref, value in zip(outs[3 * who : 3 * who + 3], new):
                    out_ref[...] = value


def update(scales, squares, state, grads, old_params, old_moments, peer_grads, bound):
    layers, own, columns = state[0].shape
    width = grads[0].shape[-1]
    count = len(grads)
    size = block_of(width, 12288)
    per, blocks = width // size, columns // size
    shape = (layers, own, size)

    def part(first, many, row=0):
        return pl.BlockSpec(shape, lambda i: (row, 0, jnp.clip(i - first, 0, many - 1)))

    return pl.pallas_call(
        functools.partial(update_kernel, count, bound),
        grid=(blocks,),
        in_specs=[
            pl.BlockSpec(memory_space=pltpu.SMEM),
            pl.BlockSpec(squares.shape, lambda i: (0, 0)),
        ]
        + [part(0, blocks)] * 4
        + [part(0, blocks, row) for row in range(2)]
        + [part(k * per, per) for k in range(count)] * 2,
        out_specs=[part(0, blocks)] * 6,
        out_shape=[jax.ShapeDtypeStruct((layers, own, columns), jnp.float32)] * 6,
        compiler_params=room,
        cost_estimate=cost_of(*[state[0]] * 14),
        name="update",
    )(scales, squares, *state, old_params, *[old_moments] * 2, *grads, *peer_grads)


def joined_kernel(*refs):
    *parts, out_ref = refs
    layers = parts[0].shape[0]
    for index, part_ref in enumerate(parts):
        out_ref[index * layers : (index + 1) * layers] = part_ref[...]


def joined(arrays):
    layers, own, columns = arrays[0].shape
    size = block_of(columns, 12288)
    return pl.pallas_call(
        joined_kernel,
        grid=(columns // size,),
        in_specs=[pl.BlockSpec((layers, own, size), lambda i: (0, 0, i))] * len(arrays),
        out_specs=pl.BlockSpec((len(arrays) * layers, own, size), lambda i: (0, 0, i)),
        out_shape=jax.ShapeDtypeStruct((len(arrays) * layers, own, columns), jnp.float32),
        compiler_params=room,
        cost_estimate=cost_of(*arrays, *arrays),
        name="joined",
    )(*arrays)


def total_of(value, later, last):
    peers, groups = lax.axis_size("dp"), lax.axis_size("mp")
    if peers & (peers - 1) or groups & (groups - 1) or peers < 4:
        return lax.psum(value, ("dp", "mp")), later, last

    def exchanged(value, axis, members, bit):
        return value + lax.ppermute(value, axis, [(i, i ^ bit) for i in members])

    value = exchanged(value, "dp", range(peers), 1)
    value, later = lax.optimization_barrier((value, later))
    value = exchanged(value, "dp", range(peers), 2)
    value, last = lax.optimization_barrier((value, last))
    first = [i for i in range(peers) if not i & 2]
    bit = 4
    while bit < peers:
        value = exchanged(value, "dp", first, bit)
        bit *= 2
    bit = 1
    while bit < groups:
        value = exchanged(value, "mp", range(groups), bit)
        bit *= 2
    passed = lax.ppermute(value, "dp", [(i, i | 2) for i in first])
    return jnp.where(lax.axis_index("dp") & 2 == 0, value, passed), later, last


def local(acc_grads, activations, cotangent, params, first_moment, second_moment, step):
    _, layers, rows, columns = acc_grads.shape
    tokens = activations.shape[0]
    peers = lax.axis_size("dp")
    chips = peers // 2
    half = chips // 2
    order = [2 * z for z in range(half)] + [2 * z + 1 for z in reversed(range(half))]

    def hop(by):
        return [
            (2 * order[r] + core, 2 * order[(r + by) % chips] + core)
            for r in range(chips)
            for core in range(2)
        ]

    swap = [(i, i ^ 1) for i in range(peers)]
    onward = [(i, (i + 1) % peers) for i in range(peers)]

    index = lax.axis_index("dp")
    core, chip = index % 2, index // 2
    place = jnp.where(chip % 2 == 0, chip // 2, chips - 1 - chip // 2)
    hops = jnp.arange(half + 1, dtype=jnp.int32)
    tables = [
        jnp.concatenate([jnp.mod(place + by * hops, chips), core.reshape(1)]) for by in (1, -1)
    ]

    state = (params, first_moment, second_moment)
    old_params = lax.ppermute(params, "dp", onward)
    moments = joined(state[1:])
    old_moments = lax.ppermute(moments, "dp", onward)

    same = jnp.eye(layers, dtype=activations.dtype)
    inputs = activations.transpose(1, 2, 0)[:, :, :, None] * same[:, None, None, :]
    inputs = inputs.reshape(layers * rows, tokens * layers)

    width = columns // streams
    keep, theirs, sent = ([None] * streams for _ in range(3))
    for k in range(streams):
        keep[k], *gives = make_terms(
            core.reshape(1), inputs, acc_grads, cotangent, order, k * width, width,
            [[moments], [old_params], []][min(k, 2)],
        )
        theirs[k] = [lax.ppermute(give, "dp", swap) for give in gives]
    for k in range(streams):
        total = shard_sum(
            plain_kernel, tables[0], half, keep[k], theirs[k]
        )
        sent[k] = [None, None]
        sent[k][k % 2] = lax.ppermute(total, "dp", hop(-1 if k % 2 else 1))
    waiting = [old_moments]
    for away in range(half - 1, 0, -1):
        for k in range(streams):
            for way, by in enumerate((1, -1)):
                arrived = [] if sent[k][way] is None else [sent[k][way]]
                body = step_kernel if arrived else plain_kernel
                after = []
                if arrived:
                    after, waiting = waiting, after
                total = shard_sum(
                    body, tables[way], away, keep[k], theirs[k], *arrived, after=after
                )
                sent[k][way] = lax.ppermute(total, "dp", hop(by))
    ours = [shard_sum(plain_kernel, tables[0], 0, keep[k], theirs[k]) for k in range(streams)]
    grads, squares = last_sums(ours, sent)
    squares, *waiting = total_of(squares, grads[1:], grads[:1])
    peer_grads = [lax.ppermute(value, "dp", onward) for value in waiting[1] + waiting[0]]
    bound = float((layers * rows * columns * lax.axis_size("mp")) ** 0.5)
    count = step.astype(jnp.float32)
    scales = jnp.concatenate(
        [
            1.0 - jnp.power(jnp.float32(beta_one), count),
            1.0 - jnp.power(jnp.float32(beta_two), count),
        ]
    )
    return tuple(update(scales, squares, state, grads, old_params, old_moments, peer_grads, bound))


def solution(mesh):
    owned = P(None, "dp", "mp")
    return jax.shard_map(
        local,
        mesh=mesh,
        in_specs=(
            P("dp", None, None, "mp"),
            P("dp", None, None),
            P("dp", None, "mp"),
            owned,
            owned,
            owned,
            P(),
        ),
        out_specs=(owned,) * 6,
        check_vma=False,
    )
```

```python
import functools
import math

import jax
import jax.numpy as jnp
from jax import lax
from jax.experimental import pallas as pl
from jax.experimental.pallas import tpu as pltpu
from jax.sharding import PartitionSpec as P

beta_one = 0.9
beta_two = 0.95
learn_rate = 0.1
decay_rate = 0.1
epsilon = 1e-08

streams = 2
lanes = 128
room = pltpu.CompilerParams(vmem_limit_bytes=64*2**20)


def block_of(columns, most):
    best = lanes
    for size in range(lanes, min(columns, most) + 1, lanes):
        if columns % size == 0:
            best = size
    return best


def cost_of(*arrays):
    moved = sum(math.prod(a.shape) * jnp.dtype(a.dtype).itemsize for a in arrays)
    return pl.CostEstimate(flops=0, bytes_accessed=moved, transcendentals=0)


def adamw_update(weights, first, second, grad, factor, first_scale, second_scale):
    scaled = factor * grad
    first_new = beta_one * first + (1.0 - beta_one) * scaled
    second_new = beta_two * second + (1.0 - beta_two) * scaled * scaled
    first_hat = first_new / first_scale
    second_hat = second_new / second_scale
    weights_new = weights - learn_rate * (
        first_hat / (jnp.sqrt(second_hat) + epsilon) + decay_rate * weights
    )
    return (weights_new, first_new, second_new)


def terms_kernel(order, layers, core_ref, inputs_ref, earlier_ref, outgrad_ref, *rest):
    keep_ref, gives = rest[-1 - layers], rest[-layers:]
    core = core_ref[0]
    tokens, _, columns = outgrad_ref.shape
    rows = earlier_ref.shape[2]
    outgrad = outgrad_ref[...].reshape(tokens * layers, columns)
    product = jnp.dot(inputs_ref[...], outgrad, preferred_element_type=jnp.float32)
    chips = len(order)
    for layer in range(layers):
        total = earlier_ref[0, layer].astype(jnp.float32) + product[layer * rows : (layer + 1) * rows]
        term = total.astype(jnp.bfloat16).astype(jnp.float32)
        term = term.reshape(chips, 2, rows // (2 * chips), columns)
        for place, chip in enumerate(order):
            keep_ref[place, layer] = jnp.where(core == 0, term[chip, 0], term[chip, 1])
            gives[layer][place] = jnp.where(core == 0, term[chip, 1], term[chip, 0])


def make_terms(core, inputs, earlier, outgrad, order, start, width):
    _, layers, rows, _ = earlier.shape
    tokens = outgrad.shape[0]
    chips = len(order)
    own = rows // (2 * chips)
    size = block_of(width, 6144)
    first = start // size
    return pl.pallas_call(
        functools.partial(terms_kernel, order, layers),
        grid_spec=pltpu.PrefetchScalarGridSpec(
            num_scalar_prefetch=1,
            grid=(width // size,),
            in_specs=[
                pl.BlockSpec(inputs.shape, lambda i, core: (0, 0)),
                pl.BlockSpec((1, layers, rows, size), lambda i, core: (0, 0, 0, first + i)),
                pl.BlockSpec((tokens, layers, size), lambda i, core: (0, 0, first + i)),
            ],
            out_specs=[pl.BlockSpec((chips, layers, own, size), lambda i, core: (0, 0, 0, i))]
            + [pl.BlockSpec((chips, own, size), lambda i, core: (0, 0, i))] * layers,
        ),
        out_shape=[jax.ShapeDtypeStruct((chips, layers, own, width), jnp.float32)]
        + [jax.ShapeDtypeStruct((chips, own, width), jnp.float32)] * layers,
        compiler_params=room,
        cost_estimate=cost_of(
            jax.ShapeDtypeStruct((layers, rows + tokens, width), earlier.dtype),
            jax.ShapeDtypeStruct((layers, rows, width), jnp.float32),
        ),
        name="terms",
    )(core, inputs, earlier, outgrad)


def both_cores(keep_ref, theirs):
    return jnp.stack([keep_ref[0, layer] + theirs_ref[0] for layer, theirs_ref in enumerate(theirs)])


def plain_kernel(layers, shard_ref, keep_ref, *rest):
    theirs, out_ref = rest[:layers], rest[-1]
    out_ref[...] = both_cores(keep_ref, theirs)


def step_kernel(layers, shard_ref, keep_ref, *rest):
    theirs, arrived_ref, out_ref = rest[:layers], rest[layers], rest[-1]
    out_ref[...] = arrived_ref[...] + both_cores(keep_ref, theirs)


def last_kernel(streams, *refs):
    *refs, squares_ref = refs
    refs, outs = refs[:-streams], refs[-streams:]
    step = pl.program_id(0)
    per = pl.num_programs(0) // streams

    @pl.when(step == 0)
    def _():
        squares_ref[...] = jnp.zeros_like(squares_ref)

    for k in range(streams):

        @pl.when(step // per == k)
        def _(k=k):
            own_ref, up_ref, down_ref = refs[3 * k : 3 * k + 3]
            grad = (up_ref[...] + down_ref[...]) + own_ref[...]
            outs[k][...] = grad
            layers, own, columns = grad.shape
            squares = (grad * grad).reshape(layers, own, columns // lanes, lanes)
            squares_ref[...] += jnp.sum(squares, axis=(0, 2))


def last_sums(ours, sent):
    streams = len(ours)
    layers, own, width = ours[0].shape
    size = block_of(width, 12288)
    per = width // size
    specs = [
        pl.BlockSpec(
            (layers, own, size), lambda i, k=k: (0, 0, jnp.clip(i - k * per, 0, per - 1))
        )
        for k in range(streams)
    ]
    summed = jax.ShapeDtypeStruct(ours[0].shape, jnp.float32)
    *grads, squares = pl.pallas_call(
        functools.partial(last_kernel, streams),
        grid=(streams * per,),
        in_specs=[spec for spec in specs for _ in range(3)],
        out_specs=specs + [pl.BlockSpec((own, lanes), lambda i: (0, 0))],
        out_shape=[summed] * streams + [jax.ShapeDtypeStruct((own, lanes), jnp.float32)],
        compiler_params=room,
        cost_estimate=cost_of(*[summed] * (4 * streams)),
        name="last_sums",
    )(*[array for k in range(streams) for array in (ours[k], *sent[k])])
    return grads, squares


def shard_sum(body, shards, which, keep, theirs, *arrived, after=()):
    _, layers, own, width = keep.shape
    size = block_of(width, 6144)
    chosen = pl.BlockSpec((1, layers, own, size), lambda i, shards: (shards[which], 0, 0, i))
    layer = pl.BlockSpec((1, own, size), lambda i, shards: (shards[which], 0, i))
    whole = pl.BlockSpec((layers, own, size), lambda i, shards: (0, 0, i))
    summed = jax.ShapeDtypeStruct((layers, own, width), jnp.float32)
    return pl.pallas_call(
        functools.partial(body, layers),
        grid_spec=pltpu.PrefetchScalarGridSpec(
            num_scalar_prefetch=1,
            grid=(width // size,),
            in_specs=[chosen]
            + [layer] * layers
            + [whole] * len(arrived)
            + [pl.BlockSpec(memory_space=pl.ANY)] * len(after),
            out_specs=whole,
        ),
        out_shape=summed,
        compiler_params=room,
        cost_estimate=cost_of(*[summed] * (3 + len(arrived))),
        name="shard_sum",
    )(shards, keep, *theirs, *arrived, *after)


def update_kernel(count, bound, scales_ref, squares_ref, passed_ref, *rest):
    states, grads, outs = (rest[:3], rest[3:6]), rest[6 : 6 + 2 * count], rest[6 + 2 * count :]
    step = pl.program_id(0)
    per = pl.num_programs(0) // count
    squares = jnp.where(scales_ref[2] == 0.0, squares_ref[...], passed_ref[...])
    factor = jnp.minimum(
        jnp.float32(1.0), bound / (jnp.sqrt(jnp.sum(squares)) + jnp.float32(1e-06))
    )
    for index in range(count):

        @pl.when(step // per == index)
        def _(index=index):
            for who in range(2):
                new = adamw_update(
                    *[ref[...] for ref in states[who]],
                    grads[who * count + index][...],
                    factor,
                    scales_ref[0],
                    scales_ref[1],
                )
                for out_ref, value in zip(outs[3 * who : 3 * who + 3], new):
                    out_ref[...] = value


def update(scales, squares, state, grads, old_copy, peer_grads, bound):
    layers, own, columns = state[0].shape
    width = grads[0].shape[-1]
    count = len(grads)
    size = block_of(width, 12288)
    per, blocks = width // size, columns // size
    shape = (layers, own, size)

    def part(first, many, row=0):
        return pl.BlockSpec(shape, lambda i: (row, 0, jnp.clip(i - first, 0, many - 1)))

    return pl.pallas_call(
        functools.partial(update_kernel, count, bound),
        grid=(blocks,),
        in_specs=[
            pl.BlockSpec(memory_space=pltpu.SMEM),
        ]
        + [pl.BlockSpec(squares[0].shape, lambda i: (0, 0))] * 2
        + [part(0, blocks)] * 3
        + [part(0, blocks, row) for row in range(3)]
        + [part(k * per, per) for k in range(count)] * 2,
        out_specs=[part(0, blocks)] * 6,
        out_shape=[jax.ShapeDtypeStruct((layers, own, columns), jnp.float32)] * 6,
        compiler_params=room,
        cost_estimate=cost_of(*[state[0]] * 14),
        name="update",
    )(scales, *squares, *state, *[old_copy] * 3, *grads, *peer_grads)


def joined_kernel(*refs):
    *parts, out_ref = refs
    layers = parts[0].shape[0]
    for index, part_ref in enumerate(parts):
        out_ref[index * layers : (index + 1) * layers] = part_ref[...]


def joined(arrays):
    layers, own, columns = arrays[0].shape
    size = block_of(columns, 12288)
    return pl.pallas_call(
        joined_kernel,
        grid=(columns // size,),
        in_specs=[pl.BlockSpec((layers, own, size), lambda i: (0, 0, i))] * len(arrays),
        out_specs=pl.BlockSpec((len(arrays) * layers, own, size), lambda i: (0, 0, i)),
        out_shape=jax.ShapeDtypeStruct((len(arrays) * layers, own, columns), jnp.float32),
        compiler_params=room,
        cost_estimate=cost_of(*arrays, *arrays),
        name="joined",
    )(*arrays)


def total_of(value, later, last):
    peers, groups = lax.axis_size("dp"), lax.axis_size("mp")
    if peers & (peers - 1) or groups & (groups - 1) or peers < 4:
        total = lax.psum(value, ("dp", "mp"))
        return (total, total), later, last

    def exchanged(value, axis, members, bit):
        return value + lax.ppermute(value, axis, [(i, i ^ bit) for i in members])

    value = exchanged(value, "dp", range(peers), 1)
    value, later = lax.optimization_barrier((value, later))
    value = exchanged(value, "dp", range(peers), 2)
    value, last = lax.optimization_barrier((value, last))
    first = [i for i in range(peers) if not i & 2]
    bit = 4
    while bit < peers:
        value = exchanged(value, "dp", first, bit)
        bit *= 2
    bit = 1
    while bit < groups:
        value = exchanged(value, "mp", range(groups), bit)
        bit *= 2
    passed = lax.ppermute(value, "dp", [(i, i | 2) for i in first])
    return (value, passed), later, last


def local(acc_grads, activations, cotangent, params, first_moment, second_moment, step):
    _, layers, rows, columns = acc_grads.shape
    tokens = activations.shape[0]
    peers = lax.axis_size("dp")
    chips = peers // 2
    half = chips // 2
    order = [2 * z for z in range(half)] + [2 * z + 1 for z in reversed(range(half))]

    def hop(by):
        return [
            (2 * order[r] + core, 2 * order[(r + by) % chips] + core)
            for r in range(chips)
            for core in range(2)
        ]

    swap = [(i, i ^ 1) for i in range(peers)]
    onward = [(i, (i + 1) % peers) for i in range(peers)]

    index = lax.axis_index("dp")
    core, chip = index % 2, index // 2
    place = jnp.where(chip % 2 == 0, chip // 2, chips - 1 - chip // 2)
    hops = jnp.arange(half + 1, dtype=jnp.int32)
    tables = [
        jnp.concatenate([jnp.mod(place + by * hops, chips), core.reshape(1)]) for by in (1, -1)
    ]

    state = (params, first_moment, second_moment)
    old_copy = lax.ppermute(joined(state), "dp", onward)

    same = jnp.eye(layers, dtype=activations.dtype)
    inputs = activations.transpose(1, 2, 0)[:, :, :, None] * same[:, None, None, :]
    inputs = inputs.reshape(layers * rows, tokens * layers)

    width = columns // streams
    keep, theirs, sent = ([None] * streams for _ in range(3))
    for k in range(streams):
        keep[k], *gives = make_terms(
            core.reshape(1), inputs, acc_grads, cotangent, order, k * width, width
        )
        theirs[k] = [lax.ppermute(give, "dp", swap) for give in gives]
    for k in range(streams):
        total = shard_sum(
            plain_kernel, tables[0], half, keep[k], theirs[k]
        )
        sent[k] = [None, None]
        sent[k][k % 2] = lax.ppermute(total, "dp", hop(-1 if k % 2 else 1))
    waiting = [old_copy]
    for away in range(half - 1, 0, -1):
        for k in range(streams):
            for way, by in enumerate((1, -1)):
                arrived = [] if sent[k][way] is None else [sent[k][way]]
                body = step_kernel if arrived else plain_kernel
                after = []
                if arrived:
                    after, waiting = waiting, after
                total = shard_sum(
                    body, tables[way], away, keep[k], theirs[k], *arrived, after=after
                )
                sent[k][way] = lax.ppermute(total, "dp", hop(by))
    ours = [shard_sum(plain_kernel, tables[0], 0, keep[k], theirs[k]) for k in range(streams)]
    grads, squares = last_sums(ours, sent)
    squares, *waiting = total_of(squares, grads[1:], grads[:1])
    peer_grads = [lax.ppermute(value, "dp", onward) for value in waiting[1] + waiting[0]]
    bound = float((layers * rows * columns * lax.axis_size("mp")) ** 0.5)
    count = step.astype(jnp.float32)
    scales = jnp.concatenate(
        [
            1.0 - jnp.power(jnp.float32(beta_one), count),
            1.0 - jnp.power(jnp.float32(beta_two), count),
            (chip % 2).astype(jnp.float32).reshape(1),
        ]
    )
    return tuple(update(scales, squares, state, grads, old_copy, peer_grads, bound))


def solution(mesh):
    owned = P(None, "dp", "mp")
    return jax.shard_map(
        local,
        mesh=mesh,
        in_specs=(
            P("dp", None, None, "mp"),
            P("dp", None, None),
            P("dp", None, "mp"),
            owned,
            owned,
            owned,
            P(),
        ),
        out_specs=(owned,) * 6,
        check_vma=False,
    )
```

```python
import functools
import math

import jax
import jax.numpy as jnp
from jax import lax
from jax.experimental import pallas as pl
from jax.experimental.pallas import tpu as pltpu
from jax.sharding import PartitionSpec as P

beta_one = 0.9
beta_two = 0.95
learn_rate = 0.1
decay_rate = 0.1
epsilon = 1e-08

streams = 2
lanes = 128
room = pltpu.CompilerParams(vmem_limit_bytes=64*2**20)


def block_of(columns, most):
    best = lanes
    for size in range(lanes, min(columns, most) + 1, lanes):
        if columns % size == 0:
            best = size
    return best


def cost_of(*arrays):
    moved = sum(math.prod(a.shape) * jnp.dtype(a.dtype).itemsize for a in arrays)
    return pl.CostEstimate(flops=0, bytes_accessed=moved, transcendentals=0)


def adamw_update(weights, first, second, grad, factor, first_scale, second_scale):
    scaled = factor * grad
    first_new = beta_one * first + (1.0 - beta_one) * scaled
    second_new = beta_two * second + (1.0 - beta_two) * scaled * scaled
    first_hat = first_new / first_scale
    second_hat = second_new / second_scale
    weights_new = weights - learn_rate * (
        first_hat / (jnp.sqrt(second_hat) + epsilon) + decay_rate * weights
    )
    return (weights_new, first_new, second_new)


def terms_kernel(order, layers, core_ref, inputs_ref, earlier_ref, outgrad_ref, *rest):
    keep_ref, gives = rest[-1 - layers], rest[-layers:]
    core = core_ref[0]
    tokens, _, columns = outgrad_ref.shape
    rows = earlier_ref.shape[2]
    outgrad = outgrad_ref[...].reshape(tokens * layers, columns)
    product = jnp.dot(inputs_ref[...], outgrad, preferred_element_type=jnp.float32)
    chips = len(order)
    for layer in range(layers):
        total = earlier_ref[0, layer].astype(jnp.float32) + product[layer * rows : (layer + 1) * rows]
        term = total.astype(jnp.bfloat16).astype(jnp.float32)
        term = term.reshape(chips, 2, rows // (2 * chips), columns)
        for place, chip in enumerate(order):
            keep_ref[place, layer] = jnp.where(core == 0, term[chip, 0], term[chip, 1])
            gives[layer][place] = jnp.where(core == 0, term[chip, 1], term[chip, 0])


def make_terms(core, inputs, earlier, outgrad, order, start, width):
    _, layers, rows, _ = earlier.shape
    tokens = outgrad.shape[0]
    chips = len(order)
    own = rows // (2 * chips)
    size = block_of(width, 6144)
    first = start // size
    return pl.pallas_call(
        functools.partial(terms_kernel, order, layers),
        grid_spec=pltpu.PrefetchScalarGridSpec(
            num_scalar_prefetch=1,
            grid=(width // size,),
            in_specs=[
                pl.BlockSpec(inputs.shape, lambda i, core: (0, 0)),
                pl.BlockSpec((1, layers, rows, size), lambda i, core: (0, 0, 0, first + i)),
                pl.BlockSpec((tokens, layers, size), lambda i, core: (0, 0, first + i)),
            ],
            out_specs=[pl.BlockSpec((chips, layers, own, size), lambda i, core: (0, 0, 0, i))]
            + [pl.BlockSpec((chips, own, size), lambda i, core: (0, 0, i))] * layers,
        ),
        out_shape=[jax.ShapeDtypeStruct((chips, layers, own, width), jnp.float32)]
        + [jax.ShapeDtypeStruct((chips, own, width), jnp.float32)] * layers,
        compiler_params=room,
        cost_estimate=cost_of(
            jax.ShapeDtypeStruct((layers, rows + tokens, width), earlier.dtype),
            jax.ShapeDtypeStruct((layers, rows, width), jnp.float32),
        ),
        name="terms",
    )(core, inputs, earlier, outgrad)


def both_cores(keep_ref, theirs):
    return jnp.stack([keep_ref[0, layer] + theirs_ref[0] for layer, theirs_ref in enumerate(theirs)])


def plain_kernel(layers, shard_ref, keep_ref, *rest):
    theirs, out_ref = rest[:layers], rest[-1]
    out_ref[...] = both_cores(keep_ref, theirs)


def step_kernel(layers, shard_ref, keep_ref, *rest):
    theirs, arrived_ref, out_ref = rest[:layers], rest[layers], rest[-1]
    out_ref[...] = arrived_ref[...] + both_cores(keep_ref, theirs)


def last_kernel(streams, *refs):
    *refs, squares_ref = refs
    refs, outs = refs[:-streams], refs[-streams:]
    step = pl.program_id(0)
    per = pl.num_programs(0) // streams

    @pl.when(step == 0)
    def _():
        squares_ref[...] = jnp.zeros_like(squares_ref)

    for k in range(streams):

        @pl.when(step // per == k)
        def _(k=k):
            own_ref, up_ref, down_ref = refs[3 * k : 3 * k + 3]
            grad = (up_ref[...] + down_ref[...]) + own_ref[...]
            outs[k][...] = grad
            layers, own, columns = grad.shape
            squares = (grad * grad).reshape(layers, own, columns // lanes, lanes)
            squares_ref[...] += jnp.sum(squares, axis=(0, 2))


def last_sums(ours, sent):
    streams = len(ours)
    layers, own, width = ours[0].shape
    size = block_of(width, 12288)
    per = width // size
    specs = [
        pl.BlockSpec(
            (layers, own, size), lambda i, k=k: (0, 0, jnp.clip(i - k * per, 0, per - 1))
        )
        for k in range(streams)
    ]
    summed = jax.ShapeDtypeStruct(ours[0].shape, jnp.float32)
    *grads, squares = pl.pallas_call(
        functools.partial(last_kernel, streams),
        grid=(streams * per,),
        in_specs=[spec for spec in specs for _ in range(3)],
        out_specs=specs + [pl.BlockSpec((own, lanes), lambda i: (0, 0))],
        out_shape=[summed] * streams + [jax.ShapeDtypeStruct((own, lanes), jnp.float32)],
        compiler_params=room,
        cost_estimate=cost_of(*[summed] * (4 * streams)),
        name="last_sums",
    )(*[array for k in range(streams) for array in (ours[k], *sent[k])])
    return grads, squares


def shard_sum(body, shards, which, keep, theirs, *arrived, after=()):
    _, layers, own, width = keep.shape
    size = block_of(width, 6144)
    chosen = pl.BlockSpec((1, layers, own, size), lambda i, shards: (shards[which], 0, 0, i))
    layer = pl.BlockSpec((1, own, size), lambda i, shards: (shards[which], 0, i))
    whole = pl.BlockSpec((layers, own, size), lambda i, shards: (0, 0, i))
    summed = jax.ShapeDtypeStruct((layers, own, width), jnp.float32)
    return pl.pallas_call(
        functools.partial(body, layers),
        grid_spec=pltpu.PrefetchScalarGridSpec(
            num_scalar_prefetch=1,
            grid=(width // size,),
            in_specs=[chosen]
            + [layer] * layers
            + [whole] * len(arrived)
            + [pl.BlockSpec(memory_space=pl.ANY)] * len(after),
            out_specs=whole,
        ),
        out_shape=summed,
        compiler_params=room,
        cost_estimate=cost_of(*[summed] * (3 + len(arrived))),
        name="shard_sum",
    )(shards, keep, *theirs, *arrived, *after)


def update_kernel(count, bound, scales_ref, squares_ref, passed_ref, *rest):
    states, grads, outs = (rest[:3], rest[3:6]), rest[6 : 6 + 2 * count], rest[6 + 2 * count :]
    step = pl.program_id(0)
    per = pl.num_programs(0) // count
    squares = jnp.where(scales_ref[2] == 0.0, squares_ref[...], passed_ref[...])
    factor = jnp.minimum(
        jnp.float32(1.0), bound / (jnp.sqrt(jnp.sum(squares)) + jnp.float32(1e-06))
    )
    for index in range(count):

        @pl.when(step // per == index)
        def _(index=index):
            for who in range(2):
                new = adamw_update(
                    *[ref[...] for ref in states[who]],
                    grads[who * count + index][...],
                    factor,
                    scales_ref[0],
                    scales_ref[1],
                )
                for out_ref, value in zip(outs[3 * who : 3 * who + 3], new):
                    out_ref[...] = value


def update(scales, squares, state, grads, old_copy, peer_grads, bound):
    layers, own, columns = state[0].shape
    width = grads[0].shape[-1]
    count = len(grads)
    size = block_of(width, 12288)
    per, blocks = width // size, columns // size
    shape = (layers, own, size)

    def part(first, many, row=0):
        return pl.BlockSpec(shape, lambda i: (row, 0, jnp.clip(i - first, 0, many - 1)))

    return pl.pallas_call(
        functools.partial(update_kernel, count, bound),
        grid=(blocks,),
        in_specs=[
            pl.BlockSpec(memory_space=pltpu.SMEM),
        ]
        + [pl.BlockSpec(squares[0].shape, lambda i: (0, 0))] * 2
        + [part(0, blocks)] * 3
        + [part(0, blocks, row) for row in range(3)]
        + [part(k * per, per) for k in range(count)] * 2,
        out_specs=[part(0, blocks)] * 6,
        out_shape=[jax.ShapeDtypeStruct((layers, own, columns), jnp.float32)] * 6,
        compiler_params=room,
        cost_estimate=cost_of(*[state[0]] * 14),
        name="update",
    )(scales, *squares, *state, *[old_copy] * 3, *grads, *peer_grads)


def joined_kernel(*refs):
    *parts, out_ref = refs
    layers = parts[0].shape[0]
    for index, part_ref in enumerate(parts):
        out_ref[index * layers : (index + 1) * layers] = part_ref[...]


def joined(arrays):
    layers, own, columns = arrays[0].shape
    size = block_of(columns, 12288)
    return pl.pallas_call(
        joined_kernel,
        grid=(columns // size,),
        in_specs=[pl.BlockSpec((layers, own, size), lambda i: (0, 0, i))] * len(arrays),
        out_specs=pl.BlockSpec((len(arrays) * layers, own, size), lambda i: (0, 0, i)),
        out_shape=jax.ShapeDtypeStruct((len(arrays) * layers, own, columns), jnp.float32),
        compiler_params=room,
        cost_estimate=cost_of(*arrays, *arrays),
        name="joined",
    )(*arrays)


def total_of(value, later, last):
    peers, groups = lax.axis_size("dp"), lax.axis_size("mp")
    if peers & (peers - 1) or groups & (groups - 1) or peers < 4:
        total = lax.psum(value, ("dp", "mp"))
        return (total, total), later, last

    def exchanged(value, axis, members, bit):
        return value + lax.ppermute(value, axis, [(i, i ^ bit) for i in members])

    value = exchanged(value, "dp", range(peers), 1)
    value, later = lax.optimization_barrier((value, later))
    value = exchanged(value, "dp", range(peers), 2)
    value, last = lax.optimization_barrier((value, last))
    first = [i for i in range(peers) if not i & 2]
    bit = 4
    while bit < peers:
        value = exchanged(value, "dp", first, bit)
        bit *= 2
    bit = 1
    while bit < groups:
        value = exchanged(value, "mp", range(groups), bit)
        bit *= 2
    passed = lax.ppermute(value, "dp", [(i, i | 2) for i in first])
    return (value, passed), later, last


def local(acc_grads, activations, cotangent, params, first_moment, second_moment, step):
    _, layers, rows, columns = acc_grads.shape
    tokens = activations.shape[0]
    peers = lax.axis_size("dp")
    chips = peers // 2
    half = chips // 2
    order = [2 * z for z in range(half)] + [2 * z + 1 for z in reversed(range(half))]

    def hop(by):
        return [
            (2 * order[r] + core, 2 * order[(r + by) % chips] + core)
            for r in range(chips)
            for core in range(2)
        ]

    swap = [(i, i ^ 1) for i in range(peers)]
    onward = [(i, (i + 1) % peers) for i in range(peers)]

    index = lax.axis_index("dp")
    core, chip = index % 2, index // 2
    place = jnp.where(chip % 2 == 0, chip // 2, chips - 1 - chip // 2)
    hops = jnp.arange(half + 1, dtype=jnp.int32)
    tables = [
        jnp.concatenate([jnp.mod(place + by * hops, chips), core.reshape(1)]) for by in (1, -1)
    ]

    state = (params, first_moment, second_moment)
    old_copy = lax.ppermute(joined(state), "dp", onward)

    same = jnp.eye(layers, dtype=activations.dtype)
    inputs = activations.transpose(1, 2, 0)[:, :, :, None] * same[:, None, None, :]
    inputs = inputs.reshape(layers * rows, tokens * layers)

    width = columns // streams
    keep, theirs, sent = ([None] * streams for _ in range(3))
    for k in range(streams):
        keep[k], *gives = make_terms(
            core.reshape(1), inputs, acc_grads, cotangent, order, k * width, width
        )
        theirs[k] = [lax.ppermute(give, "dp", swap) for give in gives]
    for k in range(streams):
        total = shard_sum(
            plain_kernel, tables[0], half, keep[k], theirs[k]
        )
        sent[k] = [None, None]
        sent[k][k % 2] = lax.ppermute(total, "dp", hop(-1 if k % 2 else 1))
    waiting = [old_copy]
    for away in range(half - 1, 0, -1):
        for k in range(streams):
            for way, by in enumerate((1, -1)):
                arrived = [] if sent[k][way] is None else [sent[k][way]]
                body = step_kernel if arrived else plain_kernel
                after = []
                if arrived:
                    after, waiting = waiting, after
                total = shard_sum(
                    body, tables[way], away, keep[k], theirs[k], *arrived, after=after
                )
                sent[k][way] = lax.ppermute(total, "dp", hop(by))
    ours = [shard_sum(plain_kernel, tables[0], 0, keep[k], theirs[k]) for k in range(streams)]
    grads, squares = last_sums(ours, sent)
    squares, *waiting = total_of(squares, [], grads)
    peer_grads = [lax.ppermute(value, "dp", onward) for value in waiting[0] + waiting[1]]
    bound = float((layers * rows * columns * lax.axis_size("mp")) ** 0.5)
    count = step.astype(jnp.float32)
    scales = jnp.concatenate(
        [
            1.0 - jnp.power(jnp.float32(beta_one), count),
            1.0 - jnp.power(jnp.float32(beta_two), count),
            (chip % 2).astype(jnp.float32).reshape(1),
        ]
    )
    return tuple(update(scales, squares, state, grads, old_copy, peer_grads, bound))


def solution(mesh):
    owned = P(None, "dp", "mp")
    return jax.shard_map(
        local,
        mesh=mesh,
        in_specs=(
            P("dp", None, None, "mp"),
            P("dp", None, None),
            P("dp", None, "mp"),
            owned,
            owned,
            owned,
            P(),
        ),
        out_specs=(owned,) * 6,
        check_vma=False,
    )
```
